512 devices in a mesh: dp: 32 (over z, x_hi), seq: 16 (over y, x_lo, core).
Axes of the slice: x: 4 (x_hi: 2, x_lo: 2; x = x_hi * 2 + x_lo), y: 4, z: 16, core: 2. Of those that a mesh axis runs over, the one named last changes fastest.
Arguments:
- queries: bfloat16 [32, 4096, 1024], P('dp', 'seq'), may hold values from -6 to 6
- keys: bfloat16 [32, 4096, 1024], P('dp', 'seq'), may hold values from -6 to 6
- values: bfloat16 [32, 4096, 1024], P('dp', 'seq'), may hold values from -6 to 6
- out_grad: bfloat16 [32, 4096, 1024], P('dp', 'seq'), may hold values from -6 to 6
- out_weight: bfloat16 [1024, 1024], P(('dp', 'seq')), may hold values from -0.1875 to 0.1875
- layout: int32 [32, 4], replicated, may hold values from 0 to 31, as said below
Outputs:
- mixed: bfloat16 [32, 4096, 1024], P('dp', 'seq')
- query_grad: bfloat16 [32, 4096, 1024], P('dp', 'seq')
- key_grad: bfloat16 [32, 4096, 1024], P('dp', 'seq')
- value_grad: bfloat16 [32, 4096, 1024], P('dp', 'seq')
- weight_grad: float32 [1024, 1024], P(('dp', 'seq'))
The draws below stay inside these ranges and needn't reach their ends.
Inputs may be any that keep to these rules, and one draw needn't show every extreme that they name: `layout`: row b lists 4 distinct blocks, the first being b.
All inputs are finite; a program needn't handle non-finite values.
Results may differ from the reference program's by a relative error of at most 0.015.
Values may be sent and summed in bfloat16 or wider, within the bound.
No kernel may reach another device: no remote copies, remote signals or barrier semaphores. Data moves between devices by JAX's collectives and lax.ppermute only.
A program may use at most 64 MiB of HBM per device.

```python
import math
import jax
import jax.numpy as jnp
from jax import lax

D = 1024
H = 16
E = 64
KB = 4
LENGTH = 4096
NQB = 32
SCENES = 32


def draw_queries(key, part):
    field = jnp.clip(jax.random.normal(jax.random.fold_in(key, 1), (SCENES, LENGTH, D), jnp.float32), -6.0, 6.0)
    return field.astype(jnp.bfloat16)


def draw_keys(key, part):
    field = jnp.clip(jax.random.normal(jax.random.fold_in(key, 2), (SCENES, LENGTH, D), jnp.float32), -6.0, 6.0)
    return field.astype(jnp.bfloat16)


def draw_layout(key, part):
    row_ids = jnp.arange(NQB).astype(jnp.int32)
    row_keys = jax.random.split(jax.random.fold_in(key, 11), NQB)

    def pick_offsets(row_key):
        return jax.random.permutation(row_key, NQB - 1)[:KB - 1].astype(jnp.int32) + 1
    offsets = jax.vmap(pick_offsets)(row_keys)
    others = (row_ids[:, None] + offsets) % NQB
    return jnp.concatenate([row_ids[:, None], others], axis=1).astype(jnp.int32)


def shard_levels(own_key, shape, cuts, low, high):
    def one(position, shards_of):
        heights = jax.random.uniform(jax.random.fold_in(jax.random.fold_in(own_key, 6), position), (shards_of,), jnp.float32, low / len(cuts), high / len(cuts))
        return jnp.repeat(jnp.exp(heights), shape[position] // shards_of).reshape((-1,) + (1,) * (len(shape) - position - 1))

    level = one(*cuts[0])
    for cut in cuts[1:]:
        level = level * one(*cut)
    return level


def gaussian(stream_key, dims, deviation, bound, cuts=(), dtype=jnp.bfloat16):
    values = deviation * jax.random.normal(stream_key, dims, jnp.float32)
    if cuts:
        values = values * shard_levels(stream_key, dims, cuts, -0.22, 0.18)
    return jnp.clip(values, -bound, bound).astype(dtype)


def setup_inputs(seed: int = 0) -> dict:
    key_list = jax.random.split(jax.random.key(seed), 7)
    return {
        "queries": draw_queries(jax.random.fold_in(key_list[6], 71), 0),
        "keys": draw_keys(jax.random.fold_in(key_list[6], 71), 0),
        "values": gaussian(key_list[2], (SCENES, LENGTH, D), 1.0, 6.0, ((0, 32), (1, 16))),
        "out_grad": gaussian(key_list[3], (SCENES, LENGTH, D), 1.0, 6.0, ((0, 32), (1, 16))),
        "out_weight": gaussian(key_list[4], (D, D), D ** -0.5, 0.1875, ((0, 512),)),
        "layout": draw_layout(jax.random.fold_in(key_list[6], 71), 0),
    }


def sparse_attention(query, keyset, values, grad_out, layout):
    seq_len, head_count, head_size = query.shape
    block_count, per_row = layout.shape
    block_len = seq_len // block_count
    scale = 1.0 / math.sqrt(head_size)
    group_shape = (block_count // 4, 4, block_len, head_count, head_size)
    key_blocks = keyset.reshape(block_count, block_len, head_count, head_size)
    value_blocks = values.reshape(block_count, block_len, head_count, head_size)
    block_ids = jnp.arange(block_count).astype(jnp.int32)

    def per_group(totals, pieces):
        key_total, value_total = totals
        query_group, grad_group, chosen = pieces
        flat_ids = chosen.reshape(-1).astype(jnp.int32)
        key_sel = jnp.take(key_blocks, flat_ids, axis=0).reshape(4, per_row * block_len, head_count, head_size)
        value_sel = jnp.take(value_blocks, flat_ids, axis=0).reshape(4, per_row * block_len, head_count, head_size)
        query_wide = query_group.astype(jnp.float32)
        grad_wide = grad_group.astype(jnp.float32)
        key_wide = key_sel.astype(jnp.float32)
        value_wide = value_sel.astype(jnp.float32)
        scores = jnp.einsum('gqhe,gkhe->ghqk', query_wide, key_wide) * scale
        top = lax.optimization_barrier(jnp.max(scores, axis=-1, keepdims=True))
        expo = jnp.exp(scores - top)
        probs = expo / lax.optimization_barrier(jnp.sum(expo, axis=-1, keepdims=True))
        probs_low = probs.astype(jnp.bfloat16)
        attended = jnp.einsum('ghqk,gkhe->gqhe', probs_low.astype(jnp.float32), value_wide).astype(jnp.bfloat16)
        dprob = jnp.einsum('gqhe,gkhe->ghqk', grad_wide, value_wide)
        inner = lax.optimization_barrier(jnp.sum(probs * dprob, axis=-1, keepdims=True))
        dscore = (probs * (dprob - inner) * scale).astype(jnp.bfloat16)
        grad_query = jnp.einsum('ghqk,gkhe->gqhe', dscore.astype(jnp.float32), key_wide).astype(jnp.bfloat16)
        key_part = jnp.einsum('ghqk,gqhe->gkhe', dscore.astype(jnp.float32), query_wide)
        value_part = jnp.einsum('ghqk,gqhe->gkhe', probs_low.astype(jnp.float32), grad_wide)
        key_part = key_part.reshape(4 * per_row, block_len * head_count * head_size)
        value_part = value_part.reshape(4 * per_row, block_len * head_count * head_size)
        onehot = (flat_ids[:, None] == block_ids[None, :]).astype(jnp.float32)
        key_total = key_total + jnp.dot(onehot.T, key_part, precision=lax.Precision.HIGHEST)
        value_total = value_total + jnp.dot(onehot.T, value_part, precision=lax.Precision.HIGHEST)
        return ((key_total, value_total), (attended, grad_query))
    zeros = jnp.zeros((block_count, block_len * head_count * head_size), jnp.float32)
    totals, outputs = lax.scan(per_group, (zeros, zeros), (query.reshape(group_shape), grad_out.reshape(group_shape), layout.reshape(block_count // 4, 4, per_row)))
    attended = outputs[0].reshape(seq_len, head_count, head_size)
    grad_query = outputs[1].reshape(seq_len, head_count, head_size)
    grad_key = totals[0].reshape(seq_len, head_count, head_size).astype(jnp.bfloat16)
    grad_value = totals[1].reshape(seq_len, head_count, head_size).astype(jnp.bfloat16)
    return (attended, grad_query, grad_key, grad_value)

def reference(queries, keys, values, out_grad, out_weight, layout):
    split_shape = (LENGTH, H, E)

    def per_scene(weight_total, pieces):
        query_rows, key_rows, value_rows, grad_rows = pieces
        grad_attention = jnp.dot(grad_rows, out_weight.T, preferred_element_type=jnp.float32).astype(jnp.bfloat16)
        attended, grad_query, grad_key, grad_value = sparse_attention(query_rows.reshape(split_shape), key_rows.reshape(split_shape), value_rows.reshape(split_shape), grad_attention.reshape(split_shape), layout)
        attended = attended.reshape(LENGTH, D)
        mixed_rows = jnp.dot(attended, out_weight, preferred_element_type=jnp.float32).astype(jnp.bfloat16)
        weight_total = weight_total + jnp.dot(attended.T, grad_rows, preferred_element_type=jnp.float32)
        return (weight_total, (mixed_rows, grad_query.reshape(LENGTH, D), grad_key.reshape(LENGTH, D), grad_value.reshape(LENGTH, D)))
    weight_grad, outputs = lax.scan(per_scene, jnp.zeros((D, D), jnp.float32), (queries, keys, values, out_grad))
    return (outputs[0], outputs[1], outputs[2], outputs[3], weight_grad)
```

```python
import jax
import jax.numpy as jnp
from jax import lax
from jax.experimental import pallas as pl
from jax.experimental.pallas import tpu as pltpu
from jax.sharding import PartitionSpec as P

H = 16
E = 64
B = 128
BF = jnp.bfloat16
F32 = jnp.float32
NT = (((1,), (1,)), ((), ()))
NN = (((1,), (0,)), ((), ()))
TN = (((0,), (0,)), ((), ()))
VM = pl.BlockSpec(memory_space=pltpu.VMEM)
SM = pl.BlockSpec(memory_space=pltpu.SMEM)


def call(kernel, outs, in_specs, scratch=(), flops=0, moved=0):
    return pl.pallas_call(
        kernel,
        out_shape=[jax.ShapeDtypeStruct(shape, dtype) for shape, dtype in outs],
        in_specs=in_specs,
        out_specs=[VM] * len(outs),
        scratch_shapes=list(scratch),
        compiler_params=pltpu.CompilerParams(vmem_limit_bytes=48 * 2**20),
        cost_estimate=pl.CostEstimate(flops=flops, bytes_accessed=moved, transcendentals=0),
    )


def low_lanes(rows):
    return lax.broadcasted_iota(jnp.int32, (rows, 2 * E), 1) < E


def interleave(a, b):
    low = low_lanes(a.shape[0])
    return jnp.where(low, a, pltpu.roll(b, E, 1)), jnp.where(low, pltpu.roll(a, E, 1), b)


def pack_kernel(q_ref, k_ref, v_ref, qs_ref, kvs_ref):
    for pair in range(H // 2):
        cols = slice(pair * 2 * E, (pair + 1) * 2 * E)
        even, odd = interleave(q_ref[:B, cols].astype(F32), q_ref[B:, cols].astype(F32))
        qs_ref[2 * pair] = even.astype(BF)
        qs_ref[2 * pair + 1] = odd.astype(BF)
        even, odd = interleave(k_ref[:, cols].astype(F32), v_ref[:, cols].astype(F32))
        kvs_ref[2 * pair] = even.astype(BF)
        kvs_ref[2 * pair + 1] = odd.astype(BF)


def grad_kernel(og_ref, w_ref, perm_ref, gs_ref, tmp_ref):
    for quad in range(H // 4):
        rows = slice(quad * 4 * E, (quad + 1) * 4 * E)
        g = lax.dot_general(og_ref[...], w_ref[rows, :], NT, preferred_element_type=F32)
        tmp_ref[:, rows] = g.astype(BF)
    for quad in range(H // 4):
        rows = slice(quad * 4 * E, (quad + 1) * 4 * E)
        g = lax.dot_general(tmp_ref[...], perm_ref[rows, :], NT, preferred_element_type=F32)
        for i in range(2):
            part = g[:, i * 2 * E:(i + 1) * 2 * E]
            even, odd = interleave(part[:B], part[B:])
            gs_ref[4 * quad + 2 * i] = even.astype(BF)
            gs_ref[4 * quad + 2 * i + 1] = odd.astype(BF)


def attention_kernel(layout_ref, q_ref, g_ref, kv_ref, att_ref, dq_ref, dkv_ref, kvt_ref, acc_ref):
    blocks = layout_ref.shape[0]
    scale = 1.0 / E**0.5
    log2e = 1.4426950408889634

    def prepare(b, carry):
        at = pl.multiple_of(b * B, B)
        kvt_ref[b] = kv_ref[pl.ds(at, B), :].T
        acc_ref[pl.ds(at, B), :] = jnp.zeros((B, 2 * E), F32)
        return carry

    lax.fori_loop(0, blocks, prepare, 0, unroll=4)

    def per_pair(s, carry):
        at = pl.multiple_of(s * B, B)
        qt = q_ref[pl.ds(at, B), :].T
        gt = g_ref[pl.ds(at, B), :].T
        zero = jnp.zeros((E, B), BF)
        att_t, dq_t = [], []
        for p in range(2):
            ids = [layout_ref[2 * s + p, j] for j in range(4)]
            starts = [pl.multiple_of(i * B, B) for i in ids]
            rows = slice(p * E, (p + 1) * E)
            xt = jnp.concatenate(
                [
                    jnp.concatenate([qt[rows], zero], axis=1),
                    jnp.concatenate([zero, gt[rows]], axis=1),
                ],
                axis=0,
            )
            kv = jnp.concatenate([kv_ref[pl.ds(i, B), :] for i in starts], axis=0)
            both = lax.dot_general(kv, xt, NN, preferred_element_type=F32)
            scores, dprob = both[:, :B], both[:, B:]
            top = jnp.max(scores, axis=0, keepdims=True)
            expo = jnp.exp2((scores - top) * (scale * log2e))
            inverse = 1.0 / jnp.sum(expo, axis=0, keepdims=True)
            inner = jnp.sum(expo * dprob, axis=0, keepdims=True) * inverse
            probs = (expo * inverse).astype(BF)
            dscore = (expo * ((dprob - inner) * (inverse * scale))).astype(BF)
            yt = jnp.concatenate([dscore, probs], axis=1)
            kvt = jnp.concatenate([kvt_ref[i] for i in ids], axis=1)
            out = lax.dot_general(kvt, yt, NN, preferred_element_type=F32)
            dq_t.append(out[:E, :B])
            att_t.append(out[E:, B:])
            part = lax.dot_general(yt, xt, NT, preferred_element_type=F32)
            for j in range(4):
                acc_ref[pl.ds(starts[j], B), :] += part[j * B:(j + 1) * B]
        att_ref[pl.ds(at, B), :] = jnp.concatenate(att_t, axis=0).T.astype(BF)
        dq_ref[pl.ds(at, B), :] = jnp.concatenate(dq_t, axis=0).T.astype(BF)
        return carry

    lax.fori_loop(0, blocks // 2, per_pair, 0)
    dkv_ref[...] = acc_ref[...].astype(BF)


def unpack_tokens(src_ref, dst_ref):
    for pair in range(H // 2):
        cols = slice(pair * 2 * E, (pair + 1) * 2 * E)
        first, second = interleave(src_ref[2 * pair].astype(F32), src_ref[2 * pair + 1].astype(F32))
        dst_ref[:B, cols] = first.astype(BF)
        dst_ref[B:, cols] = second.astype(BF)


def project_kernel(as_ref, og_ref, w_ref, perm_ref, mixed_ref, part_ref, tmp_ref, att_ref):
    unpack_tokens(as_ref, tmp_ref)
    wide = 4 * E
    for i in range(H // 4):
        cols = slice(i * wide, (i + 1) * wide)
        att_ref[:, cols] = lax.dot_general(
            tmp_ref[...], perm_ref[:, cols], NN, preferred_element_type=F32
        ).astype(BF)
    for i in range(H // 4):
        cols = slice(i * wide, (i + 1) * wide)
        mixed_ref[:, cols] = lax.dot_general(
            att_ref[...], w_ref[:, cols], NN, preferred_element_type=F32
        ).astype(BF)
    for i in range(H // 4):
        cols = slice(i * wide, (i + 1) * wide)
        part_ref[cols, :] = lax.dot_general(
            att_ref[:, cols], og_ref[...], TN, preferred_element_type=F32
        ).astype(part_ref.dtype)


def unpack_kernel(dqs_ref, dkvs_ref, dq_ref, dk_ref, dv_ref):
    unpack_tokens(dqs_ref, dq_ref)
    for pair in range(H // 2):
        cols = slice(pair * 2 * E, (pair + 1) * 2 * E)
        dk, dv = interleave(dkvs_ref[2 * pair].astype(F32), dkvs_ref[2 * pair + 1].astype(F32))
        dk_ref[:, cols] = dk.astype(BF)
        dv_ref[:, cols] = dv.astype(BF)


def sum_kernel(parts_ref, total_ref):
    total_ref[...] = jnp.sum(parts_ref[...].astype(F32), axis=0).astype(total_ref.dtype)


def add_up(parts, dtype):
    return call(sum_kernel, [(parts.shape[1:], dtype)], [VM], moved=2 * parts.size)(parts)[0]


def attend(layout, q, g, kv):
    tokens = kv.shape[0]
    half = (tokens // 2, 2 * E)
    return call(
        attention_kernel,
        [(half, BF), (half, BF), ((tokens, 2 * E), BF)],
        [SM, VM, VM, VM],
        [pltpu.VMEM((tokens // B, 2 * E, B), BF), pltpu.VMEM((tokens, 2 * E), F32)],
        flops=12 * tokens * 512 * E,
        moved=5 * 2**20,
    )(layout, q, g, kv)


def exchange(x, axis):
    return lax.all_to_all(x, axis, split_axis=0, concat_axis=0, tiled=True)


def row_order(width, dp, seq):
    each = width // (dp * seq)
    place = lax.broadcasted_iota(jnp.int32, (width, width), 1)
    inner = place % (dp * each)
    owner = (inner // each) * seq + place // (dp * each)
    feature = lax.broadcasted_iota(jnp.int32, (width, width), 0)
    return (feature == owner * each + inner % each).astype(BF)


def gather_weight(rows, dp):
    column = exchange(jnp.tile(rows[None], (dp, 1, 1)), "dp")
    return lax.all_gather(column.reshape(-1, rows.shape[1]), "seq", axis=0, tiled=True)


def reduce_weight(part, dp, seq):
    width = part.shape[1]
    part = add_up(exchange(part.reshape(seq, -1, width), "seq"), BF)
    return exchange(part.reshape(dp, -1, width), "dp").astype(F32).sum(axis=0)


def body(dp, seq, queries, keys, values, out_grad, out_weight, layout):
    tokens, width = queries.shape[1:]
    grad = out_grad[0]
    weight = gather_weight(out_weight, dp)
    perm = row_order(width, dp, seq)
    qs, kvs = call(
        pack_kernel, [((H, B, 2 * E), BF), ((H, tokens, 2 * E), BF)], [VM] * 3, moved=3 * 2**20
    )(queries[0], keys[0], values[0])
    kv = exchange(kvs, "seq").reshape(-1, 2 * E)
    q = exchange(qs, "seq").reshape(-1, 2 * E)
    gs = call(
        grad_kernel, [((H, B, 2 * E), BF)], [VM] * 3, [pltpu.VMEM((tokens, width), BF)],
        flops=2 * tokens * width * width, moved=3 * 2**20,
    )(grad, weight, perm)[0]
    g = exchange(gs, "seq").reshape(-1, 2 * E)
    att, dq, dkv = attend(layout, q, g, kv)
    att = exchange(att.reshape(H, B, 2 * E), "seq")
    mixed, part = call(
        project_kernel, [((tokens, width), BF), ((width, width), BF)], [VM] * 4,
        [pltpu.VMEM((tokens, width), BF)] * 2,
        flops=4 * tokens * width * width, moved=6 * 2**20,
    )(att, grad, weight, perm)
    weight_grad = reduce_weight(part, dp, seq)
    dq = exchange(dq.reshape(H, B, 2 * E), "seq")
    dkv = exchange(dkv.reshape(H, 2 * B, 2 * E), "seq")
    dq, dk, dv = call(
        unpack_kernel, [((tokens, width), BF)] * 3, [VM] * 2, moved=3 * 2**20
    )(dq, dkv)
    return mixed[None], dq[None], dk[None], dv[None], weight_grad


def solution(mesh):
    rows = P("dp", "seq", None)
    split = P(("dp", "seq"), None)
    sizes = mesh.shape["dp"], mesh.shape["seq"]
    return jax.shard_map(
        lambda *args: body(*sizes, *args),
        mesh=mesh,
        in_specs=(rows, rows, rows, rows, split, P()),
        out_specs=(rows, rows, rows, rows, split),
        check_vma=False,
    )
```

```python
import functools

import jax
import jax.numpy as jnp
from jax import lax
from jax.experimental import pallas as pl
from jax.experimental.pallas import tpu as pltpu
from jax.sharding import PartitionSpec as P

H = 16
E = 64
B = 128
BF = jnp.bfloat16
F32 = jnp.float32
NT = (((1,), (1,)), ((), ()))
NN = (((1,), (0,)), ((), ()))
TN = (((0,), (0,)), ((), ()))
VM = pl.BlockSpec(memory_space=pltpu.VMEM)
SM = pl.BlockSpec(memory_space=pltpu.SMEM)


def call(kernel, outs, in_specs, scratch=(), flops=0, moved=0):
    return pl.pallas_call(
        kernel,
        out_shape=[jax.ShapeDtypeStruct(shape, dtype) for shape, dtype in outs],
        in_specs=in_specs,
        out_specs=[VM] * len(outs),
        scratch_shapes=list(scratch),
        compiler_params=pltpu.CompilerParams(vmem_limit_bytes=48 * 2**20),
        cost_estimate=pl.CostEstimate(flops=flops, bytes_accessed=moved, transcendentals=0),
    )


def low_lanes(rows):
    return lax.broadcasted_iota(jnp.int32, (rows, 2 * E), 1) < E


def interleave(a, b):
    low = low_lanes(a.shape[0])
    return jnp.where(low, a, pltpu.roll(b, E, 1)), jnp.where(low, pltpu.roll(a, E, 1), b)


def key_rows(b):
    return pl.multiple_of((b // 2) * (3 * B) + B + (b % 2) * B, B)


def pack_kernel(q_ref, k_ref, v_ref, out_ref):
    for pair in range(H // 2):
        cols = slice(pair * 2 * E, (pair + 1) * 2 * E)
        for rows, (even, odd) in (
            (slice(0, B), interleave(q_ref[:B, cols].astype(F32), q_ref[B:, cols].astype(F32))),
            (slice(B, 3 * B), interleave(k_ref[:, cols].astype(F32), v_ref[:, cols].astype(F32))),
        ):
            out_ref[2 * pair, rows] = even.astype(BF)
            out_ref[2 * pair + 1, rows] = odd.astype(BF)


def grad_kernel(og_ref, w_ref, perm_ref, att_ref, out_ref, tmp_ref):
    out_ref[:, :B] = att_ref[...]
    for quad in range(H // 4):
        rows = slice(quad * 4 * E, (quad + 1) * 4 * E)
        g = lax.dot_general(og_ref[...], w_ref[rows, :], NT, preferred_element_type=F32)
        tmp_ref[:, rows] = g.astype(BF)
    for quad in range(H // 4):
        rows = slice(quad * 4 * E, (quad + 1) * 4 * E)
        g = lax.dot_general(tmp_ref[...], perm_ref[rows, :], NT, preferred_element_type=F32)
        for i in range(2):
            part = g[:, i * 2 * E:(i + 1) * 2 * E]
            even, odd = interleave(part[:B], part[B:])
            out_ref[4 * quad + 2 * i, B:] = even.astype(BF)
            out_ref[4 * quad + 2 * i + 1, B:] = odd.astype(BF)


def forward_kernel(unroll, layout_ref, qkv_ref, att_ref, stat_ref, kvt_ref):
    blocks = layout_ref.shape[0]
    scale = 1.0 / E**0.5
    log2e = 1.4426950408889634

    def prepare(b, carry):
        kvt_ref[b] = qkv_ref[pl.ds(key_rows(b), B), :].T
        return carry

    lax.fori_loop(0, blocks, prepare, 0, unroll=4)

    def per_pair(s, carry):
        at = pl.multiple_of(s * B, B)
        qt = qkv_ref[pl.ds(pl.multiple_of(s * 3 * B, B), B), :].T
        zero = jnp.zeros((E, B), BF)
        att_t = []
        for p in range(2):
            ids = [layout_ref[2 * s + p, j] for j in range(4)]
            rhs = jnp.concatenate([qt[p * E:(p + 1) * E], zero], axis=0)
            kv = jnp.concatenate([qkv_ref[pl.ds(key_rows(i), B), :] for i in ids], axis=0)
            scores = lax.dot_general(kv, rhs, NN, preferred_element_type=F32)
            top = jnp.max(scores, axis=0, keepdims=True)
            expo = jnp.exp2((scores - top) * (scale * log2e))
            inverse = 1.0 / jnp.sum(expo, axis=0, keepdims=True)
            probs = (expo * inverse).astype(BF)
            stat_ref[2 * s + p] = jnp.concatenate([top, inverse], axis=0)
            vt = jnp.concatenate([kvt_ref[i, E:, :] for i in ids], axis=1)
            att_t.append(lax.dot_general(vt, probs, NN, preferred_element_type=F32))
        att_ref[pl.ds(at, B), :] = jnp.concatenate(att_t, axis=0).T.astype(BF)
        return carry

    lax.fori_loop(0, blocks // 2, per_pair, 0, unroll=unroll)


def backward_kernel(unroll, layout_ref, qkv_ref, attg_ref, kvt_ref, stat_ref, out_ref, acc_ref):
    blocks = layout_ref.shape[0]
    scale = 1.0 / E**0.5
    log2e = 1.4426950408889634
    acc_ref[...] = jnp.zeros(acc_ref.shape, F32)

    def per_pair(s, carry):
        at = pl.multiple_of(s * 3 * B, B)
        qt = qkv_ref[pl.ds(at, B), :].T
        gt = attg_ref[pl.ds(pl.multiple_of(s * 2 * B + B, B), B), :].T
        zero = jnp.zeros((E, B), BF)
        dq_t = []
        for p in range(2):
            ids = [layout_ref[2 * s + p, j] for j in range(4)]
            starts = [key_rows(i) for i in ids]
            rows = slice(p * E, (p + 1) * E)
            left = jnp.concatenate([qt[rows], zero], axis=0)
            right = jnp.concatenate([zero, gt[rows]], axis=0)
            kv = jnp.concatenate([qkv_ref[pl.ds(i, B), :] for i in starts], axis=0)
            xt = jnp.concatenate([left, right], axis=1)
            both = lax.dot_general(kv, xt, NN, preferred_element_type=F32)
            scores, dprob = both[:, :B], both[:, B:]
            stat = stat_ref[2 * s + p]
            expo = jnp.exp2((scores - stat[:1]) * (scale * log2e))
            inverse = stat[1:]
            inner = jnp.sum(expo * dprob, axis=0, keepdims=True) * inverse
            probs = (expo * inverse).astype(BF)
            dscore = (expo * ((dprob - inner) * (inverse * scale))).astype(BF)
            kt = jnp.concatenate([kvt_ref[i, :E, :] for i in ids], axis=1)
            dq_t.append(lax.dot_general(kt, dscore, NN, preferred_element_type=F32))
            yt = jnp.concatenate([dscore, probs], axis=1)
            part = lax.dot_general(yt, xt, NT, preferred_element_type=F32)
            for j in range(4):
                acc_ref[pl.ds(starts[j], B), :] += part[j * B:(j + 1) * B]
        out_ref[pl.ds(at, B), :] = jnp.concatenate(dq_t, axis=0).T.astype(BF)
        return carry

    lax.fori_loop(0, blocks // 2, per_pair, 0, unroll=unroll)

    def finish(s, carry):
        at = pl.multiple_of(s * 3 * B + B, B)
        out_ref[pl.ds(at, 2 * B), :] = acc_ref[pl.ds(at, 2 * B), :].astype(BF)
        return carry

    lax.fori_loop(0, blocks // 2, finish, 0, unroll=4)

def unpack_tokens(src_ref, dst_ref):
    for pair in range(H // 2):
        cols = slice(pair * 2 * E, (pair + 1) * 2 * E)
        first, second = interleave(
            src_ref[2 * pair, :B].astype(F32), src_ref[2 * pair + 1, :B].astype(F32)
        )
        dst_ref[:B, cols] = first.astype(BF)
        dst_ref[B:, cols] = second.astype(BF)


def reorder(att_ref, perm_ref, out_ref):
    for i in range(H // 4):
        cols = slice(i * 4 * E, (i + 1) * 4 * E)
        out_ref[:, cols] = lax.dot_general(
            att_ref[...], perm_ref[:, cols], NN, preferred_element_type=F32
        ).astype(BF)


def partial_kernel(attg_ref, og_ref, perm_ref, own_ref, other_ref, tmp_ref, att_ref):
    unpack_tokens(attg_ref, tmp_ref)
    reorder(tmp_ref, perm_ref, att_ref)
    half = own_ref.shape[0]
    for ref, base in ((other_ref, half), (own_ref, 0)):
        for i in range(half // (4 * E)):
            cols = slice(base + i * 4 * E, base + (i + 1) * 4 * E)
            ref[i * 4 * E:(i + 1) * 4 * E, :] = lax.dot_general(
                att_ref[:, cols], og_ref[...], TN, preferred_element_type=F32
            ).astype(BF)


def mixed_kernel(attg_ref, w_ref, perm_ref, mixed_ref, tmp_ref, att_ref):
    unpack_tokens(attg_ref, tmp_ref)
    reorder(tmp_ref, perm_ref, att_ref)
    for i in range(H // 4):
        cols = slice(i * 4 * E, (i + 1) * 4 * E)
        mixed_ref[:, cols] = lax.dot_general(
            att_ref[...], w_ref[:, cols], NN, preferred_element_type=F32
        ).astype(BF)


def add_kernel(a_ref, b_ref, out_ref):
    out_ref[...] = (a_ref[...].astype(F32) + b_ref[...].astype(F32)).astype(BF)


def unpack_kernel(src_ref, dq_ref, dk_ref, dv_ref):
    unpack_tokens(src_ref, dq_ref)
    for pair in range(H // 2):
        cols = slice(pair * 2 * E, (pair + 1) * 2 * E)
        dk, dv = interleave(
            src_ref[2 * pair, B:].astype(F32), src_ref[2 * pair + 1, B:].astype(F32)
        )
        dk_ref[:, cols] = dk.astype(BF)
        dv_ref[:, cols] = dv.astype(BF)


def sum_kernel(parts_ref, total_ref):
    total_ref[...] = jnp.sum(parts_ref[...].astype(F32), axis=0).astype(total_ref.dtype)


def add_up(parts, dtype):
    return call(sum_kernel, [(parts.shape[1:], dtype)], [VM], moved=2 * parts.size)(parts)[0]


def forward(layout, qkv):
    rows = qkv.shape[0]
    blocks = layout.shape[0]
    return call(
        functools.partial(forward_kernel, 4),
        [((rows // 3, 2 * E), BF), ((blocks, 2, B), F32), ((blocks, 2 * E, B), BF)],
        [SM, VM],
        flops=2 * rows * 512 * 128 * 2,
        moved=4 * 2**20,
    )(layout, qkv)


def backward(layout, qkv, attg, kvt, stats):
    return call(
        functools.partial(backward_kernel, 4),
        [(qkv.shape, BF)],
        [SM] + [VM] * 4,
        [pltpu.VMEM(qkv.shape, F32)],
        flops=4 * qkv.shape[0] * 512 * 128 * 2,
        moved=6 * 2**20,
    )(layout, qkv, attg, kvt, stats)[0]


def exchange(x, axis, groups=None):
    return lax.all_to_all(
        x, axis, split_axis=0, concat_axis=0, tiled=True, axis_index_groups=groups
    )


def one_hot(width, rows):
    feature = lax.broadcasted_iota(jnp.int32, (width, width), 0)
    return (feature == rows[None, :]).astype(BF)


def gathered_order(width, dp, seq):
    each = width // (dp * seq)
    place = jnp.arange(width)
    owner = (place % (dp * each) // each) * seq + place // (dp * each)
    return owner * each + place % each


def reduced_order(width, dp, seq):
    each = width // (dp * seq)
    place = jnp.arange(width)
    core = (place // (width // 2) + lax.axis_index("seq")) % 2
    inner = place % (width // 2)
    owner = (inner % (dp * each) // each) * seq + inner // (dp * each) * 2 + core
    return owner * each + place % each


def body(dp, seq, queries, keys, values, out_grad, out_weight, layout):
    tokens, width = queries.shape[1:]
    grad = out_grad[0]
    square = 2 * tokens * width * width
    scratch = [pltpu.VMEM((tokens, width), BF)]
    slabs = call(pack_kernel, [((H, 3 * B, 2 * E), BF)], [VM] * 3, moved=3 * 2**20)(
        queries[0], keys[0], values[0]
    )[0]
    column = exchange(jnp.tile(out_weight[None], (dp, 1, 1)), "dp").reshape(-1, width)
    column, slabs = lax.optimization_barrier((column, slabs))
    weight = lax.all_gather(column, "seq", axis=0, tiled=True)
    qkv = exchange(slabs, "seq").reshape(-1, 2 * E)
    att, stats, kvt = forward(layout, qkv)
    gathered = one_hot(width, gathered_order(width, dp, seq))
    reduced = one_hot(width, reduced_order(width, dp, seq))
    attg = call(
        grad_kernel, [((H, 2 * B, 2 * E), BF)], [VM] * 4, scratch, flops=2 * square, moved=6 * 2**20
    )(grad, weight, gathered, att.reshape(H, B, 2 * E))[0]
    attg = exchange(attg, "seq")
    half = (width // 2, width)
    own, other = call(
        partial_kernel, [(half, BF)] * 2, [VM] * 3, scratch * 2, flops=2 * square, moved=6 * 2**20
    )(attg, grad, reduced)
    other = lax.ppermute(other, "seq", [(i, i ^ 1) for i in range(seq)])
    own = call(add_kernel, [(half, BF)], [VM] * 2, moved=3 * 2**20)(own, other)[0]
    groups = [list(range(c, seq, 2)) for c in range(2)]
    terms = exchange(own.reshape(seq // 2, -1, width), "seq", groups)
    total = add_up(terms, BF).reshape(dp, -1, width)
    attg, total = lax.optimization_barrier((attg, total))
    total = exchange(total, "dp")
    slabs = backward(layout, qkv, attg.reshape(-1, 2 * E), kvt, stats)
    mixed = call(
        mixed_kernel, [((tokens, width), BF)], [VM] * 3, scratch * 2,
        flops=2 * square, moved=5 * 2**20,
    )(attg, weight, gathered)[0]
    slabs, total = lax.optimization_barrier((slabs, total))
    weight_grad = total.astype(F32).sum(axis=0)
    slabs = exchange(slabs.reshape(H, 3 * B, 2 * E), "seq")
    dq, dk, dv = call(unpack_kernel, [((tokens, width), BF)] * 3, [VM], moved=3 * 2**20)(slabs)
    return mixed[None], dq[None], dk[None], dv[None], weight_grad


def solution(mesh):
    rows = P("dp", "seq", None)
    split = P(("dp", "seq"), None)
    sizes = mesh.shape["dp"], mesh.shape["seq"]
    return jax.shard_map(
        lambda *args: body(*sizes, *args),
        mesh=mesh,
        in_specs=(rows, rows, rows, rows, split, P()),
        out_specs=(rows, rows, rows, rows, split),
        check_vma=False,
    )
```

```python
import functools

import jax
import jax.numpy as jnp
from jax import lax
from jax.experimental import pallas as pl
from jax.experimental.pallas import tpu as pltpu
from jax.sharding import PartitionSpec as P

H = 16
E = 64
B = 128
BF = jnp.bfloat16
F32 = jnp.float32
NT = (((1,), (1,)), ((), ()))
NN = (((1,), (0,)), ((), ()))
TN = (((0,), (0,)), ((), ()))
VM = pl.BlockSpec(memory_space=pltpu.VMEM)
SM = pl.BlockSpec(memory_space=pltpu.SMEM)


def call(kernel, outs, in_specs, scratch=(), flops=0, moved=0):
    return pl.pallas_call(
        kernel,
        out_shape=[jax.ShapeDtypeStruct(shape, dtype) for shape, dtype in outs],
        in_specs=in_specs,
        out_specs=[VM] * len(outs),
        scratch_shapes=list(scratch),
        compiler_params=pltpu.CompilerParams(vmem_limit_bytes=48 * 2**20),
        cost_estimate=pl.CostEstimate(flops=flops, bytes_accessed=moved, transcendentals=0),
    )


def low_lanes(rows):
    return lax.broadcasted_iota(jnp.int32, (rows, 2 * E), 1) < E


def interleave(a, b):
    low = low_lanes(a.shape[0])
    return jnp.where(low, a, pltpu.roll(b, E, 1)), jnp.where(low, pltpu.roll(a, E, 1), b)


def key_rows(b):
    return pl.multiple_of((b // 2) * (3 * B) + B + (b % 2) * B, B)


def pack_kernel(q_ref, k_ref, v_ref, out_ref):
    for pair in range(H // 2):
        cols = slice(pair * 2 * E, (pair + 1) * 2 * E)
        for rows, (even, odd) in (
            (slice(0, B), interleave(q_ref[:B, cols].astype(F32), q_ref[B:, cols].astype(F32))),
            (slice(B, 3 * B), interleave(k_ref[:, cols].astype(F32), v_ref[:, cols].astype(F32))),
        ):
            out_ref[2 * pair, rows] = even.astype(BF)
            out_ref[2 * pair + 1, rows] = odd.astype(BF)


def grad_kernel(og_ref, w_ref, perm_ref, out_ref, tmp_ref):
    for quad in range(H // 4):
        rows = slice(quad * 4 * E, (quad + 1) * 4 * E)
        g = lax.dot_general(og_ref[...], w_ref[rows, :], NT, preferred_element_type=F32)
        tmp_ref[:, rows] = g.astype(BF)
    for quad in range(H // 4):
        rows = slice(quad * 4 * E, (quad + 1) * 4 * E)
        g = lax.dot_general(tmp_ref[...], perm_ref[rows, :], NT, preferred_element_type=F32)
        for i in range(2):
            part = g[:, i * 2 * E:(i + 1) * 2 * E]
            even, odd = interleave(part[:B], part[B:])
            out_ref[4 * quad + 2 * i] = even.astype(BF)
            out_ref[4 * quad + 2 * i + 1] = odd.astype(BF)


def forward_kernel(unroll, layout_ref, qkv_ref, att_ref, stat_ref, kvt_ref):
    blocks = layout_ref.shape[0]
    scale = 1.0 / E**0.5
    log2e = 1.4426950408889634

    def prepare(b, carry):
        kvt_ref[b] = qkv_ref[pl.ds(key_rows(b), B), :].T
        return carry

    lax.fori_loop(0, blocks, prepare, 0, unroll=4)

    def per_pair(s, carry):
        at = pl.multiple_of(s * B, B)
        qt = qkv_ref[pl.ds(pl.multiple_of(s * 3 * B, B), B), :].T
        zero = jnp.zeros((E, B), BF)
        att_t = []
        for p in range(2):
            ids = [layout_ref[2 * s + p, j] for j in range(4)]
            rhs = jnp.concatenate([qt[p * E:(p + 1) * E], zero], axis=0)
            kv = jnp.concatenate([qkv_ref[pl.ds(key_rows(i), B), :] for i in ids], axis=0)
            scores = lax.dot_general(kv, rhs, NN, preferred_element_type=F32)
            top = jnp.max(scores, axis=0, keepdims=True)
            expo = jnp.exp2((scores - top) * (scale * log2e))
            inverse = 1.0 / jnp.sum(expo, axis=0, keepdims=True)
            probs = (expo * inverse).astype(BF)
            stat_ref[2 * s + p] = jnp.concatenate([top, inverse], axis=0)
            vt = jnp.concatenate([kvt_ref[i, E:, :] for i in ids], axis=1)
            att_t.append(lax.dot_general(vt, probs, NN, preferred_element_type=F32))
        att_ref[pl.ds(at, B), :] = jnp.concatenate(att_t, axis=0).T.astype(BF)
        return carry

    lax.fori_loop(0, blocks // 2, per_pair, 0, unroll=unroll)


def backward_kernel(unroll, layout_ref, qkv_ref, g_ref, kvt_ref, stat_ref, out_ref, acc_ref):
    blocks = layout_ref.shape[0]
    scale = 1.0 / E**0.5
    log2e = 1.4426950408889634
    acc_ref[...] = jnp.zeros(acc_ref.shape, F32)

    def per_pair(s, carry):
        at = pl.multiple_of(s * 3 * B, B)
        qt = qkv_ref[pl.ds(at, B), :].T
        gt = g_ref[pl.ds(pl.multiple_of(s * B, B), B), :].T
        zero = jnp.zeros((E, B), BF)
        dq_t = []
        for p in range(2):
            ids = [layout_ref[2 * s + p, j] for j in range(4)]
            starts = [key_rows(i) for i in ids]
            rows = slice(p * E, (p + 1) * E)
            left = jnp.concatenate([qt[rows], zero], axis=0)
            right = jnp.concatenate([zero, gt[rows]], axis=0)
            kv = jnp.concatenate([qkv_ref[pl.ds(i, B), :] for i in starts], axis=0)
            xt = jnp.concatenate([left, right], axis=1)
            both = lax.dot_general(kv, xt, NN, preferred_element_type=F32)
            scores, dprob = both[:, :B], both[:, B:]
            stat = stat_ref[2 * s + p]
            expo = jnp.exp2((scores - stat[:1]) * (scale * log2e))
            inverse = stat[1:]
            inner = jnp.sum(expo * dprob, axis=0, keepdims=True) * inverse
            probs = (expo * inverse).astype(BF)
            dscore = (expo * ((dprob - inner) * (inverse * scale))).astype(BF)
            kt = jnp.concatenate([kvt_ref[i, :E, :] for i in ids], axis=1)
            dq_t.append(lax.dot_general(kt, dscore, NN, preferred_element_type=F32))
            yt = jnp.concatenate([dscore, probs], axis=1)
            part = lax.dot_general(yt, xt, NT, preferred_element_type=F32)
            for j in range(4):
                acc_ref[pl.ds(starts[j], B), :] += part[j * B:(j + 1) * B]
        out_ref[pl.ds(at, B), :] = jnp.concatenate(dq_t, axis=0).T.astype(BF)
        return carry

    lax.fori_loop(0, blocks // 2, per_pair, 0, unroll=unroll)

    def finish(s, carry):
        at = pl.multiple_of(s * 3 * B + B, B)
        out_ref[pl.ds(at, 2 * B), :] = acc_ref[pl.ds(at, 2 * B), :].astype(BF)
        return carry

    lax.fori_loop(0, blocks // 2, finish, 0, unroll=4)

def unpack_tokens(src_ref, dst_ref):
    for pair in range(H // 2):
        cols = slice(pair * 2 * E, (pair + 1) * 2 * E)
        first, second = interleave(
            src_ref[2 * pair, :B].astype(F32), src_ref[2 * pair + 1, :B].astype(F32)
        )
        dst_ref[:B, cols] = first.astype(BF)
        dst_ref[B:, cols] = second.astype(BF)


def reorder(att_ref, perm_ref, out_ref):
    for i in range(H // 4):
        cols = slice(i * 4 * E, (i + 1) * 4 * E)
        out_ref[:, cols] = lax.dot_general(
            att_ref[...], perm_ref[:, cols], NN, preferred_element_type=F32
        ).astype(BF)


def partial_kernel(att_in_ref, og_ref, perm_ref, own_ref, other_ref, tmp_ref, att_ref):
    unpack_tokens(att_in_ref, tmp_ref)
    reorder(tmp_ref, perm_ref, att_ref)
    half = own_ref.shape[0]
    for ref, base in ((other_ref, half), (own_ref, 0)):
        for i in range(half // (4 * E)):
            cols = slice(base + i * 4 * E, base + (i + 1) * 4 * E)
            ref[i * 4 * E:(i + 1) * 4 * E, :] = lax.dot_general(
                att_ref[:, cols], og_ref[...], TN, preferred_element_type=F32
            ).astype(BF)


def mixed_kernel(att_in_ref, w_ref, perm_ref, mixed_ref, tmp_ref, att_ref):
    unpack_tokens(att_in_ref, tmp_ref)
    reorder(tmp_ref, perm_ref, att_ref)
    for i in range(H // 4):
        cols = slice(i * 4 * E, (i + 1) * 4 * E)
        mixed_ref[:, cols] = lax.dot_general(
            att_ref[...], w_ref[:, cols], NN, preferred_element_type=F32
        ).astype(BF)


def add_kernel(a_ref, b_ref, out_ref):
    out_ref[...] = (a_ref[...].astype(F32) + b_ref[...].astype(F32)).astype(BF)


def unpack_kernel(src_ref, dq_ref, dk_ref, dv_ref):
    unpack_tokens(src_ref, dq_ref)
    for pair in range(H // 2):
        cols = slice(pair * 2 * E, (pair + 1) * 2 * E)
        dk, dv = interleave(
            src_ref[2 * pair, B:].astype(F32), src_ref[2 * pair + 1, B:].astype(F32)
        )
        dk_ref[:, cols] = dk.astype(BF)
        dv_ref[:, cols] = dv.astype(BF)


def sum_kernel(parts_ref, total_ref):
    total_ref[...] = jnp.sum(parts_ref[...].astype(F32), axis=0).astype(total_ref.dtype)


def add_up(parts, dtype):
    return call(sum_kernel, [(parts.shape[1:], dtype)], [VM], moved=2 * parts.size)(parts)[0]


def forward(layout, qkv):
    rows = qkv.shape[0]
    blocks = layout.shape[0]
    return call(
        functools.partial(forward_kernel, 4),
        [((rows // 3, 2 * E), BF), ((blocks, 2, B), F32), ((blocks, 2 * E, B), BF)],
        [SM, VM],
        flops=2 * rows * 512 * 128 * 2,
        moved=4 * 2**20,
    )(layout, qkv)


def backward(layout, qkv, g, kvt, stats):
    return call(
        functools.partial(backward_kernel, 4),
        [(qkv.shape, BF)],
        [SM] + [VM] * 4,
        [pltpu.VMEM(qkv.shape, F32)],
        flops=4 * qkv.shape[0] * 512 * 128 * 2,
        moved=6 * 2**20,
    )(layout, qkv, g, kvt, stats)[0]


def exchange(x, axis, groups=None):
    return lax.all_to_all(
        x, axis, split_axis=0, concat_axis=0, tiled=True, axis_index_groups=groups
    )


def one_hot(width, rows):
    feature = lax.broadcasted_iota(jnp.int32, (width, width), 0)
    return (feature == rows[None, :]).astype(BF)


def gathered_order(width, dp, seq):
    each = width // (dp * seq)
    place = jnp.arange(width)
    owner = (place % (dp * each) // each) * seq + place // (dp * each)
    return owner * each + place % each


def reduced_order(width, dp, seq):
    each = width // (dp * seq)
    place = jnp.arange(width)
    core = (place // (width // 2) + lax.axis_index("seq")) % 2
    inner = place % (width // 2)
    owner = (inner % (dp * each) // each) * seq + inner // (dp * each) * 2 + core
    return owner * each + place % each


def body(dp, seq, queries, keys, values, out_grad, out_weight, layout):
    tokens, width = queries.shape[1:]
    grad = out_grad[0]
    square = 2 * tokens * width * width
    scratch = [pltpu.VMEM((tokens, width), BF)]
    slabs = call(pack_kernel, [((H, 3 * B, 2 * E), BF)], [VM] * 3, moved=3 * 2**20)(
        queries[0], keys[0], values[0]
    )[0]
    qkv = exchange(slabs, "seq").reshape(-1, 2 * E)
    out_weight, qkv = lax.optimization_barrier((out_weight, qkv))
    column = exchange(jnp.tile(out_weight[None], (dp, 1, 1)), "dp").reshape(-1, width)
    att, stats, kvt = forward(layout, qkv)
    att, column = lax.optimization_barrier((att, column))
    weight = lax.all_gather(column, "seq", axis=0, tiled=True)
    att = exchange(att.reshape(H, B, 2 * E), "seq")
    gathered = one_hot(width, gathered_order(width, dp, seq))
    reduced = one_hot(width, reduced_order(width, dp, seq))
    half = (width // 2, width)
    own, other = call(
        partial_kernel, [(half, BF)] * 2, [VM] * 3, scratch * 2, flops=2 * square, moved=6 * 2**20
    )(att, grad, reduced)
    other = lax.ppermute(other, "seq", [(i, i ^ 1) for i in range(seq)])
    own = call(add_kernel, [(half, BF)], [VM] * 2, moved=3 * 2**20)(own, other)[0]
    groups = [list(range(c, seq, 2)) for c in range(2)]
    terms = exchange(own.reshape(seq // 2, -1, width), "seq", groups)
    total = add_up(terms, BF).reshape(dp, -1, width)
    g = call(
        grad_kernel, [((H, B, 2 * E), BF)], [VM] * 3, scratch, flops=2 * square, moved=5 * 2**20
    )(grad, weight, gathered)[0]
    g, terms = lax.optimization_barrier((g, terms))
    g = exchange(g, "seq").reshape(-1, 2 * E)
    g, total = lax.optimization_barrier((g, total))
    total = exchange(total, "dp")
    slabs = backward(layout, qkv, g, kvt, stats)
    mixed = call(
        mixed_kernel, [((tokens, width), BF)], [VM] * 3, scratch * 2,
        flops=2 * square, moved=5 * 2**20,
    )(att, weight, gathered)[0]
    slabs, total = lax.optimization_barrier((slabs, total))
    weight_grad = total.astype(F32).sum(axis=0)
    slabs = exchange(slabs.reshape(H, 3 * B, 2 * E), "seq")
    dq, dk, dv = call(unpack_kernel, [((tokens, width), BF)] * 3, [VM], moved=3 * 2**20)(slabs)
    return mixed[None], dq[None], dk[None], dv[None], weight_grad


def solution(mesh):
    rows = P("dp", "seq", None)
    split = P(("dp", "seq"), None)
    sizes = mesh.shape["dp"], mesh.shape["seq"]
    return jax.shard_map(
        lambda *args: body(*sizes, *args),
        mesh=mesh,
        in_specs=(rows, rows, rows, rows, split, P()),
        out_specs=(rows, rows, rows, rows, split),
        check_vma=False,
    )
```

```python
import functools

import jax
import jax.numpy as jnp
from jax import lax
from jax.experimental import pallas as pl
from jax.experimental.pallas import tpu as pltpu
from jax.sharding import PartitionSpec as P

H = 16
E = 64
B = 128
BF = jnp.bfloat16
F32 = jnp.float32
NT = (((1,), (1,)), ((), ()))
NN = (((1,), (0,)), ((), ()))
TN = (((0,), (0,)), ((), ()))
VM = pl.BlockSpec(memory_space=pltpu.VMEM)
SM = pl.BlockSpec(memory_space=pltpu.SMEM)


def call(kernel, outs, in_specs, scratch=(), flops=0, moved=0):
    return pl.pallas_call(
        kernel,
        out_shape=[jax.ShapeDtypeStruct(shape, dtype) for shape, dtype in outs],
        in_specs=in_specs,
        out_specs=[VM] * len(outs),
        scratch_shapes=list(scratch),
        compiler_params=pltpu.CompilerParams(vmem_limit_bytes=48 * 2**20),
        cost_estimate=pl.CostEstimate(flops=flops, bytes_accessed=moved, transcendentals=0),
    )


def low_lanes(rows):
    return lax.broadcasted_iota(jnp.int32, (rows, 2 * E), 1) < E


def interleave(a, b):
    low = low_lanes(a.shape[0])
    return jnp.where(low, a, pltpu.roll(b, E, 1)), jnp.where(low, pltpu.roll(a, E, 1), b)


def key_rows(b):
    return pl.multiple_of((b // 2) * (3 * B) + B + (b % 2) * B, B)


def pack_kernel(q_ref, k_ref, v_ref, out_ref):
    for pair in range(H // 2):
        cols = slice(pair * 2 * E, (pair + 1) * 2 * E)
        for rows, (even, odd) in (
            (slice(0, B), interleave(q_ref[:B, cols].astype(F32), q_ref[B:, cols].astype(F32))),
            (slice(B, 3 * B), interleave(k_ref[:, cols].astype(F32), v_ref[:, cols].astype(F32))),
        ):
            out_ref[2 * pair, rows] = even.astype(BF)
            out_ref[2 * pair + 1, rows] = odd.astype(BF)


def grad_kernel(og_ref, w_own_ref, w_other_ref, perm_ref, out_ref, tmp_ref):
    half = w_own_ref.shape[0]
    for i, ref in enumerate((w_own_ref, w_other_ref)):
        for at in range(0, half, 4 * E):
            g = lax.dot_general(og_ref[...], ref[at:at + 4 * E], NT, preferred_element_type=F32)
            tmp_ref[:, i * half + at:i * half + at + 4 * E] = g.astype(BF)
    for quad in range(H // 4):
        rows = slice(quad * 4 * E, (quad + 1) * 4 * E)
        g = lax.dot_general(tmp_ref[...], perm_ref[rows, :], NT, preferred_element_type=F32)
        for i in range(2):
            part = g[:, i * 2 * E:(i + 1) * 2 * E]
            even, odd = interleave(part[:B], part[B:])
            out_ref[4 * quad + 2 * i] = even.astype(BF)
            out_ref[4 * quad + 2 * i + 1] = odd.astype(BF)


def forward_kernel(unroll, layout_ref, qkv_ref, att_ref, stat_ref, kvt_ref):
    blocks = layout_ref.shape[0]
    scale = 1.0 / E**0.5
    log2e = 1.4426950408889634

    def prepare(b, carry):
        kvt_ref[b] = qkv_ref[pl.ds(key_rows(b), B), :].T
        return carry

    lax.fori_loop(0, blocks, prepare, 0, unroll=4)

    def per_pair(s, carry):
        at = pl.multiple_of(s * B, B)
        qt = qkv_ref[pl.ds(pl.multiple_of(s * 3 * B, B), B), :].T
        zero = jnp.zeros((E, B), BF)
        att_t = []
        for p in range(2):
            ids = [layout_ref[2 * s + p, j] for j in range(4)]
            rhs = jnp.concatenate([qt[p * E:(p + 1) * E], zero], axis=0)
            kv = jnp.concatenate([qkv_ref[pl.ds(key_rows(i), B), :] for i in ids], axis=0)
            scores = lax.dot_general(kv, rhs, NN, preferred_element_type=F32)
            top = jnp.max(scores, axis=0, keepdims=True)
            expo = jnp.exp2((scores - top) * (scale * log2e))
            inverse = 1.0 / jnp.sum(expo, axis=0, keepdims=True)
            probs = (expo * inverse).astype(BF)
            stat_ref[2 * s + p] = jnp.concatenate([top, inverse], axis=0)
            vt = jnp.concatenate([kvt_ref[i, E:, :] for i in ids], axis=1)
            att_t.append(lax.dot_general(vt, probs, NN, preferred_element_type=F32))
        att_ref[pl.ds(at, B), :] = jnp.concatenate(att_t, axis=0).T.astype(BF)
        return carry

    lax.fori_loop(0, blocks // 2, per_pair, 0, unroll=unroll)


def backward_kernel(unroll, layout_ref, qkv_ref, attg_ref, kvt_ref, stat_ref, out_ref, acc_ref):
    blocks = layout_ref.shape[0]
    scale = 1.0 / E**0.5
    log2e = 1.4426950408889634
    acc_ref[...] = jnp.zeros(acc_ref.shape, F32)

    def per_pair(s, carry):
        at = pl.multiple_of(s * 3 * B, B)
        qt = qkv_ref[pl.ds(at, B), :].T
        gt = attg_ref[pl.ds(pl.multiple_of(s * 2 * B + B, B), B), :].T
        zero = jnp.zeros((E, B), BF)
        dq_t = []
        for p in range(2):
            ids = [layout_ref[2 * s + p, j] for j in range(4)]
            starts = [key_rows(i) for i in ids]
            rows = slice(p * E, (p + 1) * E)
            left = jnp.concatenate([qt[rows], zero], axis=0)
            right = jnp.concatenate([zero, gt[rows]], axis=0)
            kv = jnp.concatenate([qkv_ref[pl.ds(i, B), :] for i in starts], axis=0)
            xt = jnp.concatenate([left, right], axis=1)
            both = lax.dot_general(kv, xt, NN, preferred_element_type=F32)
            scores, dprob = both[:, :B], both[:, B:]
            stat = stat_ref[2 * s + p]
            expo = jnp.exp2((scores - stat[:1]) * (scale * log2e))
            inverse = stat[1:]
            inner = jnp.sum(expo * dprob, axis=0, keepdims=True) * inverse
            probs = (expo * inverse).astype(BF)
            dscore = (expo * ((dprob - inner) * (inverse * scale))).astype(BF)
            kt = jnp.concatenate([kvt_ref[i, :E, :] for i in ids], axis=1)
            dq_t.append(lax.dot_general(kt, dscore, NN, preferred_element_type=F32))
            yt = jnp.concatenate([dscore, probs], axis=1)
            part = lax.dot_general(yt, xt, NT, preferred_element_type=F32)
            for j in range(4):
                acc_ref[pl.ds(starts[j], B), :] += part[j * B:(j + 1) * B]
        out_ref[pl.ds(at, B), :] = jnp.concatenate(dq_t, axis=0).T.astype(BF)
        return carry

    lax.fori_loop(0, blocks // 2, per_pair, 0, unroll=unroll)

    def finish(s, carry):
        at = pl.multiple_of(s * 3 * B + B, B)
        out_ref[pl.ds(at, 2 * B), :] = acc_ref[pl.ds(at, 2 * B), :].astype(BF)
        return carry

    lax.fori_loop(0, blocks // 2, finish, 0, unroll=4)

def unpack_tokens(src_ref, dst_ref):
    for pair in range(H // 2):
        cols = slice(pair * 2 * E, (pair + 1) * 2 * E)
        first, second = interleave(
            src_ref[2 * pair, :B].astype(F32), src_ref[2 * pair + 1, :B].astype(F32)
        )
        dst_ref[:B, cols] = first.astype(BF)
        dst_ref[B:, cols] = second.astype(BF)


def reorder(att_ref, perm_ref, out_ref):
    for i in range(H // 4):
        cols = slice(i * 4 * E, (i + 1) * 4 * E)
        out_ref[:, cols] = lax.dot_general(
            att_ref[...], perm_ref[:, cols], NN, preferred_element_type=F32
        ).astype(BF)


def partial_kernel(attg_ref, og_ref, perm_ref, own_ref, other_ref, att_ref, tmp_ref):
    unpack_tokens(attg_ref, tmp_ref)
    reorder(tmp_ref, perm_ref, att_ref)
    half = own_ref.shape[0]
    for ref, base in ((other_ref, half), (own_ref, 0)):
        for i in range(half // (4 * E)):
            cols = slice(base + i * 4 * E, base + (i + 1) * 4 * E)
            ref[i * 4 * E:(i + 1) * 4 * E, :] = lax.dot_general(
                att_ref[:, cols], og_ref[...], TN, preferred_element_type=F32
            ).astype(BF)


def mixed_kernel(att_ref, w_own_ref, w_other_ref, mixed_ref):
    half = w_own_ref.shape[0]
    for i in range(H // 4):
        cols = slice(i * 4 * E, (i + 1) * 4 * E)
        total = lax.dot_general(
            att_ref[:, :half], w_own_ref[:, cols], NN, preferred_element_type=F32
        )
        total += lax.dot_general(
            att_ref[:, half:], w_other_ref[:, cols], NN, preferred_element_type=F32
        )
        mixed_ref[:, cols] = total.astype(BF)


def add_kernel(a_ref, b_ref, out_ref):
    out_ref[...] = (a_ref[...].astype(F32) + b_ref[...].astype(F32)).astype(BF)


def unpack_kernel(src_ref, dq_ref, dk_ref, dv_ref):
    unpack_tokens(src_ref, dq_ref)
    for pair in range(H // 2):
        cols = slice(pair * 2 * E, (pair + 1) * 2 * E)
        dk, dv = interleave(
            src_ref[2 * pair, B:].astype(F32), src_ref[2 * pair + 1, B:].astype(F32)
        )
        dk_ref[:, cols] = dk.astype(BF)
        dv_ref[:, cols] = dv.astype(BF)


def sum_kernel(parts_ref, total_ref):
    total_ref[...] = jnp.sum(parts_ref[...].astype(F32), axis=0).astype(total_ref.dtype)


def add_up(parts, dtype):
    return call(sum_kernel, [(parts.shape[1:], dtype)], [VM], moved=2 * parts.size)(parts)[0]


def forward(layout, qkv):
    rows = qkv.shape[0]
    blocks = layout.shape[0]
    return call(
        functools.partial(forward_kernel, 4),
        [((rows // 3, 2 * E), BF), ((blocks, 2, B), F32), ((blocks, 2 * E, B), BF)],
        [SM, VM],
        flops=2 * rows * 512 * 128 * 2,
        moved=4 * 2**20,
    )(layout, qkv)


def backward(layout, qkv, attg, kvt, stats):
    return call(
        functools.partial(backward_kernel, 4),
        [(qkv.shape, BF)],
        [SM] + [VM] * 4,
        [pltpu.VMEM(qkv.shape, F32)],
        flops=4 * qkv.shape[0] * 512 * 128 * 2,
        moved=6 * 2**20,
    )(layout, qkv, attg, kvt, stats)[0]


def exchange(x, axis, groups=None):
    return lax.all_to_all(
        x, axis, split_axis=0, concat_axis=0, tiled=True, axis_index_groups=groups
    )


def one_hot(width, rows):
    feature = lax.broadcasted_iota(jnp.int32, (width, width), 0)
    return (feature == rows[None, :]).astype(BF)


def reduced_order(width, dp, seq):
    each = width // (dp * seq)
    place = jnp.arange(width)
    core = (place // (width // 2) + lax.axis_index("seq")) % 2
    inner = place % (width // 2)
    owner = (inner % (dp * each) // each) * seq + inner // (dp * each) * 2 + core
    return owner * each + place % each


def body(dp, seq, queries, keys, values, out_grad, out_weight, layout):
    tokens, width = queries.shape[1:]
    grad = out_grad[0]
    square = 2 * tokens * width * width
    scratch = [pltpu.VMEM((tokens, width), BF)]
    slabs = call(pack_kernel, [((H, 3 * B, 2 * E), BF)], [VM] * 3, moved=3 * 2**20)(
        queries[0], keys[0], values[0]
    )[0]
    perm = one_hot(width, reduced_order(width, dp, seq))
    groups = [list(range(c, seq, 2)) for c in range(2)]
    swap = [(i, i ^ 1) for i in range(seq)]
    column = exchange(jnp.tile(out_weight[None], (dp, 1, 1)), "dp").reshape(-1, width)
    column, slabs, perm = lax.optimization_barrier((column, slabs, perm))
    w_own = exchange(jnp.tile(column[None], (seq // 2, 1, 1)), "seq", groups).reshape(-1, width)
    w_own, slabs = lax.optimization_barrier((w_own, slabs))
    qkv = exchange(slabs, "seq").reshape(-1, 2 * E)
    w_other = lax.ppermute(w_own, "seq", swap)
    g = call(
        grad_kernel, [((H, B, 2 * E), BF)], [VM] * 4, scratch, flops=2 * square, moved=6 * 2**20
    )(grad, w_own, w_other, perm)[0]
    g, qkv = lax.optimization_barrier((g, qkv))
    att, stats, kvt = forward(layout, qkv)
    attg = jnp.concatenate([att.reshape(H, B, 2 * E), g], axis=1)
    attg = exchange(attg, "seq")
    half = (width // 2, width)
    own, other, att = call(
        partial_kernel, [(half, BF)] * 2 + [((tokens, width), BF)], [VM] * 3, scratch,
        flops=2 * square, moved=6 * 2**20,
    )(attg, grad, perm)
    other = lax.ppermute(other, "seq", swap)
    own = call(add_kernel, [(half, BF)], [VM] * 2, moved=3 * 2**20)(own, other)[0]
    terms = exchange(own.reshape(seq // 2, -1, width), "seq", groups)
    total = add_up(terms, BF).reshape(dp, -1, width)
    attg, total = lax.optimization_barrier((attg, total))
    total = exchange(total, "dp")
    slabs = backward(layout, qkv, attg.reshape(-1, 2 * E), kvt, stats)
    mixed = call(
        mixed_kernel, [((tokens, width), BF)], [VM] * 3, flops=square, moved=3 * 2**20
    )(att, w_own, w_other)[0]
    slabs, total = lax.optimization_barrier((slabs, total))
    weight_grad = total.astype(F32).sum(axis=0)
    slabs = exchange(slabs.reshape(H, 3 * B, 2 * E), "seq")
    dq, dk, dv = call(unpack_kernel, [((tokens, width), BF)] * 3, [VM], moved=3 * 2**20)(slabs)
    return mixed[None], dq[None], dk[None], dv[None], weight_grad


def solution(mesh):
    rows = P("dp", "seq", None)
    split = P(("dp", "seq"), None)
    sizes = mesh.shape["dp"], mesh.shape["seq"]
    return jax.shard_map(
        lambda *args: body(*sizes, *args),
        mesh=mesh,
        in_specs=(rows, rows, rows, rows, split, P()),
        out_specs=(rows, rows, rows, rows, split),
        check_vma=False,
    )
```

```python
import functools

import jax
import jax.numpy as jnp
from jax import lax
from jax.experimental import pallas as pl
from jax.experimental.pallas import tpu as pltpu
from jax.sharding import PartitionSpec as P

H = 16
E = 64
B = 128
BF = jnp.bfloat16
F32 = jnp.float32
NT = (((1,), (1,)), ((), ()))
NN = (((1,), (0,)), ((), ()))
TN = (((0,), (0,)), ((), ()))
VM = pl.BlockSpec(memory_space=pltpu.VMEM)
SM = pl.BlockSpec(memory_space=pltpu.SMEM)


def call(kernel, outs, in_specs, scratch=(), flops=0, moved=0):
    return pl.pallas_call(
        kernel,
        out_shape=[jax.ShapeDtypeStruct(shape, dtype) for shape, dtype in outs],
        in_specs=in_specs,
        out_specs=[VM] * len(outs),
        scratch_shapes=list(scratch),
        compiler_params=pltpu.CompilerParams(vmem_limit_bytes=48 * 2**20),
        cost_estimate=pl.CostEstimate(flops=flops, bytes_accessed=moved, transcendentals=0),
    )


def low_lanes(rows):
    return lax.broadcasted_iota(jnp.int32, (rows, 2 * E), 1) < E


def interleave(a, b):
    low = low_lanes(a.shape[0])
    return jnp.where(low, a, pltpu.roll(b, E, 1)), jnp.where(low, pltpu.roll(a, E, 1), b)


def key_rows(b):
    return pl.multiple_of((b // 2) * (3 * B) + B + (b % 2) * B, B)


def pack_kernel(q_ref, k_ref, v_ref, out_ref):
    for pair in range(H // 2):
        cols = slice(pair * 2 * E, (pair + 1) * 2 * E)
        for rows, (even, odd) in (
            (slice(0, B), interleave(q_ref[:B, cols].astype(F32), q_ref[B:, cols].astype(F32))),
            (slice(B, 3 * B), interleave(k_ref[:, cols].astype(F32), v_ref[:, cols].astype(F32))),
        ):
            out_ref[2 * pair, rows] = even.astype(BF)
            out_ref[2 * pair + 1, rows] = odd.astype(BF)


def grad_kernel(og_ref, w_own_ref, w_other_ref, perm_ref, out_ref, tmp_ref):
    half = w_own_ref.shape[0]
    for i, ref in enumerate((w_own_ref, w_other_ref)):
        for at in range(0, half, 4 * E):
            g = lax.dot_general(og_ref[...], ref[at:at + 4 * E], NT, preferred_element_type=F32)
            tmp_ref[:, i * half + at:i * half + at + 4 * E] = g.astype(BF)
    for quad in range(H // 4):
        rows = slice(quad * 4 * E, (quad + 1) * 4 * E)
        g = lax.dot_general(tmp_ref[...], perm_ref[rows, :], NT, preferred_element_type=F32)
        for i in range(2):
            part = g[:, i * 2 * E:(i + 1) * 2 * E]
            even, odd = interleave(part[:B], part[B:])
            out_ref[4 * quad + 2 * i] = even.astype(BF)
            out_ref[4 * quad + 2 * i + 1] = odd.astype(BF)


def forward_kernel(group, layout_ref, qkv_ref, g_ref, attg_ref, stat_ref, kvt_ref):
    blocks = layout_ref.shape[0]
    scale = 1.0 / E**0.5
    log2e = 1.4426950408889634

    def prepare(b, carry):
        kvt_ref[b] = qkv_ref[pl.ds(key_rows(b), B), :].T
        return carry

    lax.fori_loop(0, blocks, prepare, 0, unroll=8)

    def step(n, carry):
        pairs = [n * group + i for i in range(group)]
        zero = jnp.zeros((E, B), BF)
        qts = [qkv_ref[pl.ds(pl.multiple_of(s * 3 * B, B), B), :].T for s in pairs]
        work = [(s, p, [layout_ref[2 * s + p, j] for j in range(4)]) for s in pairs for p in range(2)]
        scores = []
        for i, (s, p, ids) in enumerate(work):
            rhs = jnp.concatenate([qts[i // 2][p * E:(p + 1) * E], zero], axis=0)
            kv = jnp.concatenate([qkv_ref[pl.ds(key_rows(j), B), :] for j in ids], axis=0)
            scores.append(lax.dot_general(kv, rhs, NN, preferred_element_type=F32))
        tops = [jnp.max(x, axis=0, keepdims=True) for x in scores]
        expos = [jnp.exp2((x - t) * (scale * log2e)) for x, t in zip(scores, tops)]
        inverses = [1.0 / jnp.sum(x, axis=0, keepdims=True) for x in expos]
        probs = [(x * y).astype(BF) for x, y in zip(expos, inverses)]
        outs = []
        for i, (s, p, ids) in enumerate(work):
            vt = jnp.concatenate([kvt_ref[j, E:, :] for j in ids], axis=1)
            outs.append(lax.dot_general(vt, probs[i], NN, preferred_element_type=F32))
        for i, (s, p, ids) in enumerate(work):
            stat_ref[2 * s + p] = jnp.concatenate([tops[i], inverses[i]], axis=0)
        for i, s in enumerate(pairs):
            att = jnp.concatenate([outs[2 * i], outs[2 * i + 1]], axis=0).astype(BF)
            attg_ref[s, :B] = att.T
            attg_ref[s, B:] = g_ref[s]
        return carry

    lax.fori_loop(0, blocks // 2 // group, step, 0)


def backward_kernel(
    group, layout_ref, qkv_ref, attg_ref, kvt_ref, stat_ref, out_ref, acc_ref
):
    blocks = layout_ref.shape[0]
    scale = 1.0 / E**0.5
    log2e = 1.4426950408889634
    acc_ref[...] = jnp.zeros(acc_ref.shape, F32)

    def step(n, carry):
        pairs = [n * group + i for i in range(group)]
        zero = jnp.zeros((E, B), BF)
        qts = [qkv_ref[pl.ds(pl.multiple_of(s * 3 * B, B), B), :].T for s in pairs]
        gts = [attg_ref[s, B:].T for s in pairs]
        work = [(s, p, [layout_ref[2 * s + p, j] for j in range(4)]) for s in pairs for p in range(2)]
        xts, boths = [], []
        for i, (s, p, ids) in enumerate(work):
            rows = slice(p * E, (p + 1) * E)
            left = jnp.concatenate([qts[i // 2][rows], zero], axis=0)
            right = jnp.concatenate([zero, gts[i // 2][rows]], axis=0)
            xt = jnp.concatenate([left, right], axis=1)
            kv = jnp.concatenate([qkv_ref[pl.ds(key_rows(j), B), :] for j in ids], axis=0)
            xts.append(xt)
            boths.append(lax.dot_general(kv, xt, NN, preferred_element_type=F32))
        yts = []
        for i, (s, p, ids) in enumerate(work):
            scores, dprob = boths[i][:, :B], boths[i][:, B:]
            stat = stat_ref[2 * s + p]
            expo = jnp.exp2((scores - stat[:1]) * (scale * log2e))
            inverse = stat[1:]
            inner = jnp.sum(expo * dprob, axis=0, keepdims=True) * inverse
            probs = (expo * inverse).astype(BF)
            dscore = (expo * ((dprob - inner) * (inverse * scale))).astype(BF)
            yts.append(jnp.concatenate([dscore, probs], axis=1))
        outs, parts = [], []
        for i, (s, p, ids) in enumerate(work):
            kt = jnp.concatenate([kvt_ref[j, :E, :] for j in ids], axis=1)
            outs.append(lax.dot_general(kt, yts[i][:, :B], NN, preferred_element_type=F32))
            parts.append(lax.dot_general(yts[i], xts[i], NT, preferred_element_type=F32))
        for i, (s, p, ids) in enumerate(work):
            for j in range(4):
                acc_ref[pl.ds(pl.multiple_of(ids[j] * B, B), B), :] += parts[i][j * B:(j + 1) * B]
        for i, s in enumerate(pairs):
            dq = jnp.concatenate([outs[2 * i], outs[2 * i + 1]], axis=0).astype(BF)
            out_ref[s, :B] = dq.T
        return carry

    lax.fori_loop(0, blocks // 2 // group, step, 0)

    def finish(s, carry):
        at = pl.multiple_of(s * 2 * B, B)
        out_ref[s, B:] = acc_ref[pl.ds(at, 2 * B), :].astype(BF)
        return carry

    lax.fori_loop(0, blocks // 2, finish, 0, unroll=4)

def unpack_tokens(src_ref, dst_ref):
    for pair in range(H // 2):
        cols = slice(pair * 2 * E, (pair + 1) * 2 * E)
        first, second = interleave(
            src_ref[2 * pair, :B].astype(F32), src_ref[2 * pair + 1, :B].astype(F32)
        )
        dst_ref[:B, cols] = first.astype(BF)
        dst_ref[B:, cols] = second.astype(BF)


def reorder(att_ref, perm_ref, out_ref):
    for i in range(H // 4):
        cols = slice(i * 4 * E, (i + 1) * 4 * E)
        out_ref[:, cols] = lax.dot_general(
            att_ref[...], perm_ref[:, cols], NN, preferred_element_type=F32
        ).astype(BF)


def partial_kernel(attg_ref, og_ref, perm_ref, own_ref, other_ref, att_ref, tmp_ref):
    unpack_tokens(attg_ref, tmp_ref)
    reorder(tmp_ref, perm_ref, att_ref)
    half = own_ref.shape[0]
    for ref, base in ((other_ref, half), (own_ref, 0)):
        for i in range(half // (4 * E)):
            cols = slice(base + i * 4 * E, base + (i + 1) * 4 * E)
            ref[i * 4 * E:(i + 1) * 4 * E, :] = lax.dot_general(
                att_ref[:, cols], og_ref[...], TN, preferred_element_type=F32
            ).astype(BF)


def mixed_kernel(att_ref, w_own_ref, w_other_ref, mixed_ref):
    half = w_own_ref.shape[0]
    for i in range(H // 4):
        cols = slice(i * 4 * E, (i + 1) * 4 * E)
        total = lax.dot_general(
            att_ref[:, :half], w_own_ref[:, cols], NN, preferred_element_type=F32
        )
        total += lax.dot_general(
            att_ref[:, half:], w_other_ref[:, cols], NN, preferred_element_type=F32
        )
        mixed_ref[:, cols] = total.astype(BF)


def add_kernel(a_ref, b_ref, out_ref):
    out_ref[...] = (a_ref[...].astype(F32) + b_ref[...].astype(F32)).astype(BF)


def unpack_kernel(src_ref, dq_ref, dk_ref, dv_ref):
    unpack_tokens(src_ref, dq_ref)
    for pair in range(H // 2):
        cols = slice(pair * 2 * E, (pair + 1) * 2 * E)
        dk, dv = interleave(
            src_ref[2 * pair, B:].astype(F32), src_ref[2 * pair + 1, B:].astype(F32)
        )
        dk_ref[:, cols] = dk.astype(BF)
        dv_ref[:, cols] = dv.astype(BF)


def sum_kernel(parts_ref, total_ref):
    total_ref[...] = jnp.sum(parts_ref[...].astype(F32), axis=0).astype(total_ref.dtype)


def add_up(parts, dtype):
    return call(sum_kernel, [(parts.shape[1:], dtype)], [VM], moved=2 * parts.size)(parts)[0]


def forward(layout, qkv, g):
    blocks = layout.shape[0]
    return call(
        functools.partial(forward_kernel, 4),
        [((H, 2 * B, 2 * E), BF), ((blocks, 2, B), F32), ((blocks, 2 * E, B), BF)],
        [SM, VM, VM],
        flops=2 * qkv.shape[0] * 512 * 128,
        moved=4 * 2**20,
    )(layout, qkv, g)


def backward(layout, qkv, attg, kvt, stats):
    blocks = layout.shape[0]
    return call(
        functools.partial(backward_kernel, 4),
        [((H, 3 * B, 2 * E), BF)],
        [SM] + [VM] * 4,
        [pltpu.VMEM((blocks * B, 2 * E), F32)],
        flops=4 * qkv.shape[0] * 512 * 128,
        moved=6 * 2**20,
    )(layout, qkv, attg, kvt, stats)[0]


def exchange(x, axis, groups=None):
    return lax.all_to_all(
        x, axis, split_axis=0, concat_axis=0, tiled=True, axis_index_groups=groups
    )


def one_hot(width, rows):
    feature = lax.broadcasted_iota(jnp.int32, (width, width), 0)
    return (feature == rows[None, :]).astype(BF)


def reduced_order(width, dp, seq):
    each = width // (dp * seq)
    place = jnp.arange(width)
    core = (place // (width // 2) + lax.axis_index("seq")) % 2
    inner = place % (width // 2)
    owner = (inner % (dp * each) // each) * seq + inner // (dp * each) * 2 + core
    return owner * each + place % each


def body(dp, seq, queries, keys, values, out_grad, out_weight, layout):
    tokens, width = queries.shape[1:]
    grad = out_grad[0]
    square = 2 * tokens * width * width
    scratch = [pltpu.VMEM((tokens, width), BF)]
    slabs = call(pack_kernel, [((H, 3 * B, 2 * E), BF)], [VM] * 3, moved=3 * 2**20)(
        queries[0], keys[0], values[0]
    )[0]
    perm = one_hot(width, reduced_order(width, dp, seq))
    groups = [list(range(c, seq, 2)) for c in range(2)]
    swap = [(i, i ^ 1) for i in range(seq)]
    column = exchange(jnp.tile(out_weight[None], (dp, 1, 1)), "dp").reshape(-1, width)
    column, slabs, perm = lax.optimization_barrier((column, slabs, perm))
    w_own = exchange(jnp.tile(column[None], (seq // 2, 1, 1)), "seq", groups).reshape(-1, width)
    w_own, slabs = lax.optimization_barrier((w_own, slabs))
    qkv = exchange(slabs, "seq").reshape(-1, 2 * E)
    w_other = lax.ppermute(w_own, "seq", swap)
    g = call(
        grad_kernel, [((H, B, 2 * E), BF)], [VM] * 4, scratch, flops=2 * square, moved=6 * 2**20
    )(grad, w_own, w_other, perm)[0]
    g, qkv = lax.optimization_barrier((g, qkv))
    attg, stats, kvt = forward(layout, qkv, g)
    attg = exchange(attg, "seq")
    half = (width // 2, width)
    own, other, att = call(
        partial_kernel, [(half, BF)] * 2 + [((tokens, width), BF)], [VM] * 3, scratch,
        flops=2 * square, moved=6 * 2**20,
    )(attg, grad, perm)
    other = lax.ppermute(other, "seq", swap)
    own = call(add_kernel, [(half, BF)], [VM] * 2, moved=3 * 2**20)(own, other)[0]
    terms = exchange(own.reshape(seq // 2, -1, width), "seq", groups)
    total = add_up(terms, BF).reshape(dp, -1, width)
    attg, total = lax.optimization_barrier((attg, total))
    total = exchange(total, "dp")
    slabs = backward(layout, qkv, attg, kvt, stats)
    mixed = call(
        mixed_kernel, [((tokens, width), BF)], [VM] * 3, flops=square, moved=3 * 2**20
    )(att, w_own, w_other)[0]
    slabs, total = lax.optimization_barrier((slabs, total))
    weight_grad = total.astype(F32).sum(axis=0)
    slabs = exchange(slabs, "seq")
    dq, dk, dv = call(unpack_kernel, [((tokens, width), BF)] * 3, [VM], moved=3 * 2**20)(slabs)
    return mixed[None], dq[None], dk[None], dv[None], weight_grad


def solution(mesh):
    rows = P("dp", "seq", None)
    split = P(("dp", "seq"), None)
    sizes = mesh.shape["dp"], mesh.shape["seq"]
    return jax.shard_map(
        lambda *args: body(*sizes, *args),
        mesh=mesh,
        in_specs=(rows, rows, rows, rows, split, P()),
        out_specs=(rows, rows, rows, rows, split),
        check_vma=False,
    )
```

```python
import functools

import jax
import jax.numpy as jnp
from jax import lax
from jax.experimental import pallas as pl
from jax.experimental.pallas import tpu as pltpu
from jax.sharding import PartitionSpec as P

H = 16
E = 64
B = 128
BF = jnp.bfloat16
F32 = jnp.float32
NT = (((1,), (1,)), ((), ()))
NN = (((1,), (0,)), ((), ()))
TN = (((0,), (0,)), ((), ()))
VM = pl.BlockSpec(memory_space=pltpu.VMEM)
SM = pl.BlockSpec(memory_space=pltpu.SMEM)


def call(kernel, outs, in_specs, scratch=(), flops=0, moved=0):
    return pl.pallas_call(
        kernel,
        out_shape=[jax.ShapeDtypeStruct(shape, dtype) for shape, dtype in outs],
        in_specs=in_specs,
        out_specs=[VM] * len(outs),
        scratch_shapes=list(scratch),
        compiler_params=pltpu.CompilerParams(vmem_limit_bytes=48 * 2**20),
        cost_estimate=pl.CostEstimate(flops=flops, bytes_accessed=moved, transcendentals=0),
    )


def low_lanes(rows):
    return lax.broadcasted_iota(jnp.int32, (rows, 2 * E), 1) < E


def interleave(a, b):
    low = low_lanes(a.shape[0])
    return jnp.where(low, a, pltpu.roll(b, E, 1)), jnp.where(low, pltpu.roll(a, E, 1), b)


def key_rows(b):
    return pl.multiple_of((b // 2) * (5 * B) + B + (b % 2) * B, B)


def pack_kernel(q_ref, k_ref, v_ref, out_ref):
    for pair in range(H // 2):
        cols = slice(pair * 2 * E, (pair + 1) * 2 * E)
        for rows, (even, odd) in (
            (slice(0, B), interleave(q_ref[:B, cols].astype(F32), q_ref[B:, cols].astype(F32))),
            (slice(B, 3 * B), interleave(k_ref[:, cols].astype(F32), v_ref[:, cols].astype(F32))),
        ):
            out_ref[2 * pair, rows] = even.astype(BF)
            out_ref[2 * pair + 1, rows] = odd.astype(BF)


def column_half(ref, core):
    width = ref.shape[1] // 2
    return ref[:, pl.ds(pl.multiple_of(core * width, width), width)]


def grad_kernel(core_ref, og_ref, own_ref, other_ref, perm_ref, att_ref, out_ref, w_ref, tmp_ref):
    out_ref[:, :B] = att_ref[...]
    owners, place = own_ref.shape[0], own_ref.shape[1] // 4
    for half, ref in enumerate((own_ref, other_ref)):
        for s in range(owners):
            for c in range(4):
                w_ref[s * place:(s + 1) * place, (half * 4 + c) * B:(half * 4 + c + 1) * B] = ref[
                    s, c * place:(c + 1) * place
                ]
    core = core_ref[0]
    og = jnp.concatenate([column_half(og_ref, core), column_half(og_ref, 1 - core)], axis=1)
    for quad in range(H // 4):
        rows = slice(quad * 4 * E, (quad + 1) * 4 * E)
        g = lax.dot_general(og, w_ref[rows, :], NT, preferred_element_type=F32)
        tmp_ref[:, rows] = g.astype(BF)
    for quad in range(H // 4):
        rows = slice(quad * 4 * E, (quad + 1) * 4 * E)
        g = lax.dot_general(tmp_ref[...], perm_ref[rows, :], NT, preferred_element_type=F32)
        for i in range(2):
            part = g[:, i * 2 * E:(i + 1) * 2 * E]
            even, odd = interleave(part[:B], part[B:])
            out_ref[4 * quad + 2 * i, B:] = even.astype(BF)
            out_ref[4 * quad + 2 * i + 1, B:] = odd.astype(BF)


def forward_kernel(group, layout_ref, qkv_ref, att_ref, stat_ref, kvt_ref):
    blocks = layout_ref.shape[0]
    scale = 1.0 / E**0.5
    log2e = 1.4426950408889634

    def prepare(b, carry):
        kvt_ref[b] = qkv_ref[pl.ds(key_rows(b), B), :].T
        return carry

    lax.fori_loop(0, blocks, prepare, 0, unroll=8)

    def step(n, carry):
        pairs = [n * group + i for i in range(group)]
        zero = jnp.zeros((E, B), BF)
        qts = [qkv_ref[pl.ds(pl.multiple_of(s * 5 * B, B), B), :].T for s in pairs]
        work = [(s, p, [layout_ref[2 * s + p, j] for j in range(4)]) for s in pairs for p in range(2)]
        scores = []
        for i, (s, p, ids) in enumerate(work):
            rhs = jnp.concatenate([qts[i // 2][p * E:(p + 1) * E], zero], axis=0)
            kv = jnp.concatenate([qkv_ref[pl.ds(key_rows(j), B), :] for j in ids], axis=0)
            scores.append(lax.dot_general(kv, rhs, NN, preferred_element_type=F32))
        tops = [jnp.max(x, axis=0, keepdims=True) for x in scores]
        expos = [jnp.exp2((x - t) * (scale * log2e)) for x, t in zip(scores, tops)]
        inverses = [1.0 / jnp.sum(x, axis=0, keepdims=True) for x in expos]
        probs = [(x * y).astype(BF) for x, y in zip(expos, inverses)]
        outs = []
        for i, (s, p, ids) in enumerate(work):
            vt = jnp.concatenate([kvt_ref[j, E:, :] for j in ids], axis=1)
            outs.append(lax.dot_general(vt, probs[i], NN, preferred_element_type=F32))
        for i, (s, p, ids) in enumerate(work):
            stat_ref[2 * s + p] = jnp.concatenate([tops[i], inverses[i]], axis=0)
        for i, s in enumerate(pairs):
            att = jnp.concatenate([outs[2 * i], outs[2 * i + 1]], axis=0).astype(BF)
            att_ref[s] = att.T
        return carry

    lax.fori_loop(0, blocks // 2 // group, step, 0)


def backward_kernel(
    group, layout_ref, qkv_ref, attg_ref, kvt_ref, stat_ref, out_ref, acc_ref
):
    blocks = layout_ref.shape[0]
    scale = 1.0 / E**0.5
    log2e = 1.4426950408889634
    acc_ref[...] = jnp.zeros(acc_ref.shape, F32)

    def step(n, carry):
        pairs = [n * group + i for i in range(group)]
        zero = jnp.zeros((E, B), BF)
        qts = [qkv_ref[pl.ds(pl.multiple_of(s * 5 * B, B), B), :].T for s in pairs]
        gts = [attg_ref[s, B:].T for s in pairs]
        work = [(s, p, [layout_ref[2 * s + p, j] for j in range(4)]) for s in pairs for p in range(2)]
        xts, boths = [], []
        for i, (s, p, ids) in enumerate(work):
            rows = slice(p * E, (p + 1) * E)
            left = jnp.concatenate([qts[i // 2][rows], zero], axis=0)
            right = jnp.concatenate([zero, gts[i // 2][rows]], axis=0)
            xt = jnp.concatenate([left, right], axis=1)
            kv = jnp.concatenate([qkv_ref[pl.ds(key_rows(j), B), :] for j in ids], axis=0)
            xts.append(xt)
            boths.append(lax.dot_general(kv, xt, NN, preferred_element_type=F32))
        yts = []
        for i, (s, p, ids) in enumerate(work):
            scores, dprob = boths[i][:, :B], boths[i][:, B:]
            stat = stat_ref[2 * s + p]
            expo = jnp.exp2((scores - stat[:1]) * (scale * log2e))
            inverse = stat[1:]
            inner = jnp.sum(expo * dprob, axis=0, keepdims=True) * inverse
            probs = (expo * inverse).astype(BF)
            dscore = (expo * ((dprob - inner) * (inverse * scale))).astype(BF)
            yts.append(jnp.concatenate([dscore, probs], axis=1))
        outs, parts = [], []
        for i, (s, p, ids) in enumerate(work):
            kt = jnp.concatenate([kvt_ref[j, :E, :] for j in ids], axis=1)
            outs.append(lax.dot_general(kt, yts[i][:, :B], NN, preferred_element_type=F32))
            parts.append(lax.dot_general(yts[i], xts[i], NT, preferred_element_type=F32))
        for i, (s, p, ids) in enumerate(work):
            for j in range(4):
                acc_ref[pl.ds(pl.multiple_of(ids[j] * B, B), B), :] += parts[i][j * B:(j + 1) * B]
        for i, s in enumerate(pairs):
            dq = jnp.concatenate([outs[2 * i], outs[2 * i + 1]], axis=0).astype(BF)
            out_ref[s, :B] = dq.T
        return carry

    lax.fori_loop(0, blocks // 2 // group, step, 0)

    def finish(s, carry):
        at = pl.multiple_of(s * 2 * B, B)
        out_ref[s, B:] = acc_ref[pl.ds(at, 2 * B), :].astype(BF)
        return carry

    lax.fori_loop(0, blocks // 2, finish, 0, unroll=4)

def unpack_tokens(src_ref, dst_ref):
    for pair in range(H // 2):
        cols = slice(pair * 2 * E, (pair + 1) * 2 * E)
        first, second = interleave(
            src_ref[2 * pair, :B].astype(F32), src_ref[2 * pair + 1, :B].astype(F32)
        )
        dst_ref[:B, cols] = first.astype(BF)
        dst_ref[B:, cols] = second.astype(BF)


def reorder(att_ref, perm_ref, out_ref):
    for i in range(H // 4):
        cols = slice(i * 4 * E, (i + 1) * 4 * E)
        out_ref[:, cols] = lax.dot_general(
            att_ref[...], perm_ref[:, cols], NN, preferred_element_type=F32
        ).astype(BF)


def partial_kernel(core_ref, attg_ref, og_ref, perm_ref, own_ref, other_ref, att_ref, tmp_ref):
    unpack_tokens(attg_ref, tmp_ref)
    reorder(tmp_ref, perm_ref, att_ref)
    core = core_ref[0]
    owners, place = own_ref.shape[0], own_ref.shape[1] // 4
    each = 4 * E // place
    for ref, half in ((other_ref, 1 - core), (own_ref, core)):
        og = column_half(og_ref, half)
        for i in range(owners // each):
            cols = slice(i * 4 * E, (i + 1) * 4 * E)
            part = lax.dot_general(att_ref[:, cols], og, TN, preferred_element_type=F32).astype(BF)
            for s in range(each):
                for c in range(4):
                    ref[i * each + s, c * place:(c + 1) * place] = part[
                        s * place:(s + 1) * place, c * B:(c + 1) * B
                    ]


def mixed_kernel(core_ref, att_ref, w_ref, mixed_ref):
    width = w_ref.shape[1] // 2
    for half in range(2):
        core = core_ref[0] if half == 0 else 1 - core_ref[0]
        for i in range(width // (2 * B)):
            at = half * width + i * 2 * B
            total = lax.dot_general(
                att_ref[...], w_ref[:, at:at + 2 * B], NN, preferred_element_type=F32
            )
            mixed_ref[:, pl.ds(pl.multiple_of(core * width + i * 2 * B, B), 2 * B)] = total.astype(BF)


def sum_kernel(even_ref, even2_ref, odd_ref, odd2_ref, total_ref):
    place = total_ref.shape[0]
    width = total_ref.shape[1] // 2
    for half, refs in enumerate(((even_ref, even2_ref), (odd_ref, odd2_ref))):
        for n, ref in enumerate(refs):
            total = jnp.sum(ref[:, 0].astype(F32), axis=0).astype(BF)
            for c in range(2):
                at = half * width + (2 * n + c) * B
                total_ref[:, at:at + B] = total[c * place:(c + 1) * place]


def unpack_kernel(src_ref, dq_ref, dk_ref, dv_ref):
    unpack_tokens(src_ref, dq_ref)
    for pair in range(H // 2):
        cols = slice(pair * 2 * E, (pair + 1) * 2 * E)
        dk, dv = interleave(
            src_ref[2 * pair, B:3 * B].astype(F32), src_ref[2 * pair + 1, B:3 * B].astype(F32)
        )
        dk_ref[:, cols] = dk.astype(BF)
        dv_ref[:, cols] = dv.astype(BF)


def forward(layout, qkv):
    blocks = layout.shape[0]
    return call(
        functools.partial(forward_kernel, 4),
        [((H, B, 2 * E), BF), ((blocks, 2, B), F32), ((blocks, 2 * E, B), BF)],
        [SM, VM],
        flops=4 * 2**30,
        moved=4 * 2**20,
    )(layout, qkv)


def backward(layout, qkv, attg, kvt, stats):
    blocks = layout.shape[0]
    return call(
        functools.partial(backward_kernel, 4),
        [((H, 3 * B, 2 * E), BF)],
        [SM] + [VM] * 4,
        [pltpu.VMEM((blocks * B, 2 * E), F32)],
        flops=8 * 2**30,
        moved=6 * 2**20,
    )(layout, qkv, attg, kvt, stats)[0]


def exchange(x, axis, groups=None):
    return lax.all_to_all(
        x, axis, split_axis=0, concat_axis=0, tiled=True, axis_index_groups=groups
    )


def one_hot(width, rows):
    feature = lax.broadcasted_iota(jnp.int32, (width, width), 0)
    return (feature == rows[None, :]).astype(BF)


def exchanged_order(width, dp, seq):
    each = width // (dp * seq)
    place = jnp.arange(width)
    owner = (place % (dp * each) // each) * seq + place // (dp * each)
    return owner * each + place % each


def body(dp, seq, queries, keys, values, out_grad, out_weight, layout):
    tokens, width = queries.shape[1:]
    grad = out_grad[0]
    square = 2 * tokens * width * width
    scratch = [pltpu.VMEM((tokens, width), BF)]
    core = (lax.axis_index("seq") & 1).reshape(1)
    swap = [(i, i ^ 1) for i in range(seq)]
    slabs = call(pack_kernel, [((H, 3 * B, 2 * E), BF)], [VM] * 3, moved=3 * 2**20)(
        queries[0], keys[0], values[0]
    )[0]
    perm = one_hot(width, exchanged_order(width, dp, seq))
    column = exchange(jnp.tile(out_weight[None], (dp, 1, 1)), "dp").reshape(-1, 2, 4, B)
    column, slabs, perm = lax.optimization_barrier((column, slabs, perm))
    halves = column.transpose(1, 2, 0, 3).reshape(1, 2, 2 * B, B)
    halves = jnp.tile(halves, (seq // 2, 1, 1, 1)).reshape(seq, 2 * B, B)
    slabs = exchange(jnp.concatenate([slabs, halves], axis=1), "seq")
    w_own = slabs[:, 3 * B:]
    w_other = lax.ppermute(w_own, "seq", swap)
    qkv = slabs.reshape(-1, B)
    att, stats, kvt = forward(layout, qkv)
    attg, weight = call(
        grad_kernel, [((H, 2 * B, 2 * E), BF), ((width, width), BF)], [SM] + [VM] * 5, scratch,
        flops=2 * square, moved=8 * 2**20,
    )(core, grad, w_own, w_other, perm, att)
    attg = exchange(attg, "seq")
    half = (seq, 2 * B, B)
    own, other, att = call(
        partial_kernel, [(half, BF)] * 2 + [((tokens, width), BF)], [SM] + [VM] * 3, scratch,
        flops=2 * square, moved=6 * 2**20,
    )(core, attg, grad, perm)
    other = lax.ppermute(other, "seq", swap)
    slabs = backward(layout, qkv, attg, kvt, stats)
    terms = (own.astype(F32) + other.astype(F32)).astype(BF)
    slabs = exchange(jnp.concatenate([slabs, terms], axis=1), "seq")
    pieces = slabs.reshape(seq // 2, 2, 5 * B, B)
    total = pl.pallas_call(
        sum_kernel,
        grid=(1,),
        out_shape=jax.ShapeDtypeStruct((2 * dp, width), BF),
        in_specs=[
            pl.BlockSpec((seq // 2, 1, B, B), lambda i, c=c, n=n: (0, c, 3 + n, 0))
            for c in range(2)
            for n in range(2)
        ],
        out_specs=VM,
        compiler_params=pltpu.CompilerParams(vmem_limit_bytes=48 * 2**20),
    )(pieces, pieces, pieces, pieces)
    total = exchange(total.reshape(dp, -1, width), "dp")
    mixed = call(
        mixed_kernel, [((tokens, width), BF)], [SM] + [VM] * 2, flops=square, moved=3 * 2**20
    )(core, att, weight)[0]
    mixed, slabs = lax.optimization_barrier((mixed, slabs))
    dq, dk, dv = call(unpack_kernel, [((tokens, width), BF)] * 3, [VM], moved=3 * 2**20)(slabs)
    weight_grad = total.astype(F32).sum(axis=0)
    return mixed[None], dq[None], dk[None], dv[None], weight_grad


def solution(mesh):
    rows = P("dp", "seq", None)
    split = P(("dp", "seq"), None)
    sizes = mesh.shape["dp"], mesh.shape["seq"]
    return jax.shard_map(
        lambda *args: body(*sizes, *args),
        mesh=mesh,
        in_specs=(rows, rows, rows, rows, split, P()),
        out_specs=(rows, rows, rows, rows, split),
        check_vma=False,
    )
```

```python
import functools

import jax
import jax.numpy as jnp
from jax import lax
from jax.experimental import pallas as pl
from jax.experimental.pallas import tpu as pltpu
from jax.sharding import PartitionSpec as P

H = 16
E = 64
B = 128
BF = jnp.bfloat16
F32 = jnp.float32
NT = (((1,), (1,)), ((), ()))
NN = (((1,), (0,)), ((), ()))
TN = (((0,), (0,)), ((), ()))
VM = pl.BlockSpec(memory_space=pltpu.VMEM)
SM = pl.BlockSpec(memory_space=pltpu.SMEM)


def call(kernel, outs, in_specs, scratch=(), flops=0, moved=0):
    return pl.pallas_call(
        kernel,
        out_shape=[jax.ShapeDtypeStruct(shape, dtype) for shape, dtype in outs],
        in_specs=in_specs,
        out_specs=[VM] * len(outs),
        scratch_shapes=list(scratch),
        compiler_params=pltpu.CompilerParams(vmem_limit_bytes=48 * 2**20),
        cost_estimate=pl.CostEstimate(flops=flops, bytes_accessed=moved, transcendentals=0),
    )


def low_lanes(rows):
    return lax.broadcasted_iota(jnp.int32, (rows, 2 * E), 1) < E


def interleave(a, b):
    low = low_lanes(a.shape[0])
    return jnp.where(low, a, pltpu.roll(b, E, 1)), jnp.where(low, pltpu.roll(a, E, 1), b)


def key_rows(b):
    return pl.multiple_of((b // 2) * (5 * B) + B + (b % 2) * B, B)


def pack_kernel(q_ref, k_ref, v_ref, out_ref):
    for pair in range(H // 2):
        cols = slice(pair * 2 * E, (pair + 1) * 2 * E)
        for rows, (even, odd) in (
            (slice(0, B), interleave(q_ref[:B, cols].astype(F32), q_ref[B:, cols].astype(F32))),
            (slice(B, 3 * B), interleave(k_ref[:, cols].astype(F32), v_ref[:, cols].astype(F32))),
        ):
            out_ref[2 * pair, rows] = even.astype(BF)
            out_ref[2 * pair + 1, rows] = odd.astype(BF)


def column_half(ref, core):
    width = ref.shape[1] // 2
    return ref[:, pl.ds(pl.multiple_of(core * width, width), width)]


def grad_kernel(core_ref, og_ref, own_ref, other_ref, perm_ref, att_ref, out_ref, w_ref, tmp_ref):
    out_ref[:, :B] = att_ref[...]
    owners, place = own_ref.shape[0], own_ref.shape[1] // 4
    for half, ref in enumerate((own_ref, other_ref)):
        for s in range(owners):
            for c in range(4):
                w_ref[s * place:(s + 1) * place, (half * 4 + c) * B:(half * 4 + c + 1) * B] = ref[
                    s, c * place:(c + 1) * place
                ]
    core = core_ref[0]
    og = jnp.concatenate([column_half(og_ref, core), column_half(og_ref, 1 - core)], axis=1)
    for quad in range(H // 4):
        rows = slice(quad * 4 * E, (quad + 1) * 4 * E)
        g = lax.dot_general(og, w_ref[rows, :], NT, preferred_element_type=F32)
        tmp_ref[:, rows] = g.astype(BF)
    for quad in range(H // 4):
        rows = slice(quad * 4 * E, (quad + 1) * 4 * E)
        g = lax.dot_general(tmp_ref[...], perm_ref[rows, :], NT, preferred_element_type=F32)
        for i in range(2):
            part = g[:, i * 2 * E:(i + 1) * 2 * E]
            even, odd = interleave(part[:B], part[B:])
            out_ref[4 * quad + 2 * i, B:] = even.astype(BF)
            out_ref[4 * quad + 2 * i + 1, B:] = odd.astype(BF)


def forward_kernel(group, layout_ref, qkv_ref, att_ref, stat_ref, kvt_ref):
    blocks = layout_ref.shape[0]
    scale = 1.0 / E**0.5
    log2e = 1.4426950408889634

    def prepare(b, carry):
        kvt_ref[b] = qkv_ref[pl.ds(key_rows(b), B), :].T
        return carry

    lax.fori_loop(0, blocks, prepare, 0, unroll=8)

    def step(n, carry):
        pairs = [n * group + i for i in range(group)]
        zero = jnp.zeros((E, B), BF)
        qts = [qkv_ref[pl.ds(pl.multiple_of(s * 5 * B, B), B), :].T for s in pairs]
        work = [(s, p, [layout_ref[2 * s + p, j] for j in range(4)]) for s in pairs for p in range(2)]
        scores = []
        for i, (s, p, ids) in enumerate(work):
            rhs = jnp.concatenate([qts[i // 2][p * E:(p + 1) * E], zero], axis=0)
            kv = jnp.concatenate([qkv_ref[pl.ds(key_rows(j), B), :] for j in ids], axis=0)
            scores.append(lax.dot_general(kv, rhs, NN, preferred_element_type=F32))
        tops = [jnp.max(x, axis=0, keepdims=True) for x in scores]
        expos = [jnp.exp2((x - t) * (scale * log2e)) for x, t in zip(scores, tops)]
        inverses = [1.0 / jnp.sum(x, axis=0, keepdims=True) for x in expos]
        probs = [(x * y).astype(BF) for x, y in zip(expos, inverses)]
        outs = []
        for i, (s, p, ids) in enumerate(work):
            vt = jnp.concatenate([kvt_ref[j, E:, :] for j in ids], axis=1)
            outs.append(lax.dot_general(vt, probs[i], NN, preferred_element_type=F32))
        for i, (s, p, ids) in enumerate(work):
            stat_ref[2 * s + p] = jnp.concatenate([tops[i], inverses[i]], axis=0)
        for i, s in enumerate(pairs):
            att = jnp.concatenate([outs[2 * i], outs[2 * i + 1]], axis=0).astype(BF)
            att_ref[s] = att.T
        return carry

    lax.fori_loop(0, blocks // 2 // group, step, 0)


def backward_kernel(
    group, layout_ref, qkv_ref, attg_ref, kvt_ref, stat_ref, out_ref, acc_ref
):
    blocks = layout_ref.shape[0]
    scale = 1.0 / E**0.5
    log2e = 1.4426950408889634
    acc_ref[...] = jnp.zeros(acc_ref.shape, F32)

    def step(n, carry):
        pairs = [n * group + i for i in range(group)]
        zero = jnp.zeros((E, B), BF)
        qts = [qkv_ref[pl.ds(pl.multiple_of(s * 5 * B, B), B), :].T for s in pairs]
        gts = [attg_ref[s, B:].T for s in pairs]
        work = [(s, p, [layout_ref[2 * s + p, j] for j in range(4)]) for s in pairs for p in range(2)]
        xts, boths = [], []
        for i, (s, p, ids) in enumerate(work):
            rows = slice(p * E, (p + 1) * E)
            left = jnp.concatenate([qts[i // 2][rows], zero], axis=0)
            right = jnp.concatenate([zero, gts[i // 2][rows]], axis=0)
            xt = jnp.concatenate([left, right], axis=1)
            kv = jnp.concatenate([qkv_ref[pl.ds(key_rows(j), B), :] for j in ids], axis=0)
            xts.append(xt)
            boths.append(lax.dot_general(kv, xt, NN, preferred_element_type=F32))
        yts = []
        for i, (s, p, ids) in enumerate(work):
            scores, dprob = boths[i][:, :B], boths[i][:, B:]
            stat = stat_ref[2 * s + p]
            expo = jnp.exp2((scores - stat[:1]) * (scale * log2e))
            inverse = stat[1:]
            inner = jnp.sum(expo * dprob, axis=0, keepdims=True) * inverse
            probs = (expo * inverse).astype(BF)
            dscore = (expo * ((dprob - inner) * (inverse * scale))).astype(BF)
            yts.append(jnp.concatenate([dscore, probs], axis=1))
        outs, parts = [], []
        for i, (s, p, ids) in enumerate(work):
            kt = jnp.concatenate([kvt_ref[j, :E, :] for j in ids], axis=1)
            outs.append(lax.dot_general(kt, yts[i][:, :B], NN, preferred_element_type=F32))
            parts.append(lax.dot_general(yts[i], xts[i], NT, preferred_element_type=F32))
        for i, (s, p, ids) in enumerate(work):
            for j in range(4):
                acc_ref[pl.ds(pl.multiple_of(ids[j] * B, B), B), :] += parts[i][j * B:(j + 1) * B]
        for i, s in enumerate(pairs):
            dq = jnp.concatenate([outs[2 * i], outs[2 * i + 1]], axis=0).astype(BF)
            out_ref[s, :B] = dq.T
        return carry

    lax.fori_loop(0, blocks // 2 // group, step, 0)

    def finish(s, carry):
        at = pl.multiple_of(s * 2 * B, B)
        out_ref[s, B:] = acc_ref[pl.ds(at, 2 * B), :].astype(BF)
        return carry

    lax.fori_loop(0, blocks // 2, finish, 0, unroll=4)

def unpack_tokens(src_ref, dst_ref):
    for pair in range(H // 2):
        cols = slice(pair * 2 * E, (pair + 1) * 2 * E)
        first, second = interleave(
            src_ref[2 * pair, :B].astype(F32), src_ref[2 * pair + 1, :B].astype(F32)
        )
        dst_ref[:B, cols] = first.astype(BF)
        dst_ref[B:, cols] = second.astype(BF)


def reorder(att_ref, perm_ref, out_ref):
    for i in range(H // 4):
        cols = slice(i * 4 * E, (i + 1) * 4 * E)
        out_ref[:, cols] = lax.dot_general(
            att_ref[...], perm_ref[:, cols], NN, preferred_element_type=F32
        ).astype(BF)


def partial_kernel(core_ref, attg_ref, og_ref, perm_ref, own_ref, other_ref, att_ref, tmp_ref):
    unpack_tokens(attg_ref, tmp_ref)
    reorder(tmp_ref, perm_ref, att_ref)
    core = core_ref[0]
    owners, place = own_ref.shape[0], own_ref.shape[1] // 4
    each = 4 * E // place
    for ref, half in ((other_ref, 1 - core), (own_ref, core)):
        og = column_half(og_ref, half)
        for i in range(owners // each):
            cols = slice(i * 4 * E, (i + 1) * 4 * E)
            part = lax.dot_general(att_ref[:, cols], og, TN, preferred_element_type=F32).astype(BF)
            for s in range(each):
                for c in range(4):
                    ref[i * each + s, c * place:(c + 1) * place] = part[
                        s * place:(s + 1) * place, c * B:(c + 1) * B
                    ]


def mixed_kernel(core_ref, att_ref, w_ref, mixed_ref):
    width = w_ref.shape[1] // 2
    for half in range(2):
        core = core_ref[0] if half == 0 else 1 - core_ref[0]
        for i in range(width // (2 * B)):
            at = half * width + i * 2 * B
            total = lax.dot_general(
                att_ref[...], w_ref[:, at:at + 2 * B], NN, preferred_element_type=F32
            )
            mixed_ref[:, pl.ds(pl.multiple_of(core * width + i * 2 * B, B), 2 * B)] = total.astype(BF)


def sum_kernel(even_ref, even2_ref, odd_ref, odd2_ref, total_ref):
    place = total_ref.shape[0]
    width = total_ref.shape[1] // 2
    for half, refs in enumerate(((even_ref, even2_ref), (odd_ref, odd2_ref))):
        for n, ref in enumerate(refs):
            total = jnp.sum(ref[:, 0].astype(F32), axis=0).astype(BF)
            for c in range(2):
                at = half * width + (2 * n + c) * B
                total_ref[:, at:at + B] = total[c * place:(c + 1) * place]


def unpack_kernel(src_ref, dq_ref, dk_ref, dv_ref):
    unpack_tokens(src_ref, dq_ref)
    for pair in range(H // 2):
        cols = slice(pair * 2 * E, (pair + 1) * 2 * E)
        dk, dv = interleave(
            src_ref[2 * pair, B:3 * B].astype(F32), src_ref[2 * pair + 1, B:3 * B].astype(F32)
        )
        dk_ref[:, cols] = dk.astype(BF)
        dv_ref[:, cols] = dv.astype(BF)


def forward(layout, qkv):
    blocks = layout.shape[0]
    return call(
        functools.partial(forward_kernel, 8),
        [((H, B, 2 * E), BF), ((blocks, 2, B), F32), ((blocks, 2 * E, B), BF)],
        [SM, VM],
        flops=4 * 2**30,
        moved=4 * 2**20,
    )(layout, qkv)


def backward(layout, qkv, attg, kvt, stats):
    blocks = layout.shape[0]
    return call(
        functools.partial(backward_kernel, 8),
        [((H, 3 * B, 2 * E), BF)],
        [SM] + [VM] * 4,
        [pltpu.VMEM((blocks * B, 2 * E), F32)],
        flops=8 * 2**30,
        moved=6 * 2**20,
    )(layout, qkv, attg, kvt, stats)[0]


def exchange(x, axis, groups=None):
    return lax.all_to_all(
        x, axis, split_axis=0, concat_axis=0, tiled=True, axis_index_groups=groups
    )


def one_hot(width, rows):
    feature = lax.broadcasted_iota(jnp.int32, (width, width), 0)
    return (feature == rows[None, :]).astype(BF)


def exchanged_order(width, dp, seq):
    each = width // (dp * seq)
    place = jnp.arange(width)
    owner = (place % (dp * each) // each) * seq + place // (dp * each)
    return owner * each + place % each


def body(dp, seq, queries, keys, values, out_grad, out_weight, layout):
    tokens, width = queries.shape[1:]
    grad = out_grad[0]
    square = 2 * tokens * width * width
    scratch = [pltpu.VMEM((tokens, width), BF)]
    core = (lax.axis_index("seq") & 1).reshape(1)
    swap = [(i, i ^ 1) for i in range(seq)]
    slabs = call(pack_kernel, [((H, 3 * B, 2 * E), BF)], [VM] * 3, moved=3 * 2**20)(
        queries[0], keys[0], values[0]
    )[0]
    perm = one_hot(width, exchanged_order(width, dp, seq))
    column = exchange(jnp.tile(out_weight[None], (dp, 1, 1)), "dp").reshape(-1, 2, 4, B)
    column, slabs, perm = lax.optimization_barrier((column, slabs, perm))
    halves = column.transpose(1, 2, 0, 3).reshape(1, 2, 2 * B, B)
    halves = jnp.tile(halves, (seq // 2, 1, 1, 1)).reshape(seq, 2 * B, B)
    slabs = exchange(jnp.concatenate([slabs, halves], axis=1), "seq")
    w_own = slabs[:, 3 * B:]
    w_other = lax.ppermute(w_own, "seq", swap)
    qkv = slabs.reshape(-1, B)
    att, stats, kvt = forward(layout, qkv)
    attg, weight = call(
        grad_kernel, [((H, 2 * B, 2 * E), BF), ((width, width), BF)], [SM] + [VM] * 5, scratch,
        flops=2 * square, moved=8 * 2**20,
    )(core, grad, w_own, w_other, perm, att)
    attg = exchange(attg, "seq")
    half = (seq, 2 * B, B)
    own, other, att = call(
        partial_kernel, [(half, BF)] * 2 + [((tokens, width), BF)], [SM] + [VM] * 3, scratch,
        flops=2 * square, moved=6 * 2**20,
    )(core, attg, grad, perm)
    other = lax.ppermute(other, "seq", swap)
    slabs = backward(layout, qkv, attg, kvt, stats)
    terms = (own.astype(F32) + other.astype(F32)).astype(BF)
    slabs = exchange(jnp.concatenate([slabs, terms], axis=1), "seq")
    pieces = slabs.reshape(seq // 2, 2, 5 * B, B)
    total = pl.pallas_call(
        sum_kernel,
        grid=(1,),
        out_shape=jax.ShapeDtypeStruct((2 * dp, width), BF),
        in_specs=[
            pl.BlockSpec((seq // 2, 1, B, B), lambda i, c=c, n=n: (0, c, 3 + n, 0))
            for c in range(2)
            for n in range(2)
        ],
        out_specs=VM,
        compiler_params=pltpu.CompilerParams(vmem_limit_bytes=48 * 2**20),
    )(pieces, pieces, pieces, pieces)
    total = exchange(total.reshape(dp, -1, width), "dp")
    mixed = call(
        mixed_kernel, [((tokens, width), BF)], [SM] + [VM] * 2, flops=square, moved=3 * 2**20
    )(core, att, weight)[0]
    mixed, slabs = lax.optimization_barrier((mixed, slabs))
    dq, dk, dv = call(unpack_kernel, [((tokens, width), BF)] * 3, [VM], moved=3 * 2**20)(slabs)
    weight_grad = total.astype(F32).sum(axis=0)
    return mixed[None], dq[None], dk[None], dv[None], weight_grad


def solution(mesh):
    rows = P("dp", "seq", None)
    split = P(("dp", "seq"), None)
    sizes = mesh.shape["dp"], mesh.shape["seq"]
    return jax.shard_map(
        lambda *args: body(*sizes, *args),
        mesh=mesh,
        in_specs=(rows, rows, rows, rows, split, P()),
        out_specs=(rows, rows, rows, rows, split),
        check_vma=False,
    )
```
